32 devices in a mesh: grp: 4 (over x, core), box: 8 (over z, y).
Axes of the slice: x: 2, y: 2, z: 4, core: 2. Of those that a mesh axis runs over, the one named last changes fastest.
Arguments:
- right_side: float32 [64, 256, 128], P('grp', 'box'), may hold values from -6 to 6
- beta: float32 [64, 256, 128], P('grp', 'box'), may hold values from 0.25 to 4
Outputs:
- correction: float32 [64, 256, 128], P('grp', 'box')
The draws below stay inside these ranges and needn't reach their ends.
All inputs are finite; a program needn't handle non-finite values.
Results may differ from the reference program's by a relative error of at most 0.0001.
Values sent between devices are 32-bit elements; how exact they have to be, the bound alone decides.
A program may use at most 64 MiB of HBM per device.

```python
import math
import jax
import jax.numpy as jnp

LEVELS = 4
SWEEPS = 2
COARSE = 8
NX = 64
NY = 256
NZ = 128


def draw_right_side(key, part):
    return jnp.clip(jax.random.normal(key, (NX, NY, NZ), jnp.float32), -6.0, 6.0)


def block_scale(key, dims, cuts, least, high):
    def one(axis_at, parts):
        draws = jax.random.uniform(jax.random.fold_in(jax.random.fold_in(key, 6), axis_at), (parts,), jnp.float32, least / len(cuts), high / len(cuts))
        return jnp.repeat(jnp.exp(draws), dims[axis_at] // parts).reshape((-1,) + (1,) * (len(dims) - axis_at - 1))

    level = one(*cuts[0])
    for cut in cuts[1:]:
        level = level * one(*cut)
    return level


def setup_inputs(seed: int = 0) -> dict:
    splits = jax.random.split(jax.random.key(seed), 3)
    right_side = draw_right_side(jax.random.fold_in(splits[2], 71), 0)
    beta = jnp.clip(jnp.exp(math.log(4.0) - 2.7725887 * jax.random.uniform(splits[1], (NX, NY, NZ), jnp.float32) ** block_scale(splits[1], (NX, NY, NZ), ((0, 4), (1, 8)), -0.2, 0.2)), 0.25, 4.0)
    return dict(right_side=right_side, beta=beta)


relax_weight = 2.0 / 3.0


def pad_zeros(field):
    return jnp.pad(field, 1)


def face_coeffs(padded_beta):
    face_x = 0.5 * (padded_beta[1:, 1:-1, 1:-1] + padded_beta[:-1, 1:-1, 1:-1])
    face_y = 0.5 * (padded_beta[1:-1, 1:, 1:-1] + padded_beta[1:-1, :-1, 1:-1])
    face_z = 0.5 * (padded_beta[1:-1, 1:-1, 1:] + padded_beta[1:-1, 1:-1, :-1])
    return face_x, face_y, face_z


def inverse_diagonal(coeffs, scale):
    face_x, face_y, face_z = coeffs
    total = face_x[:-1] + face_x[1:] + face_y[:, :-1] + face_y[:, 1:] + face_z[:, :, :-1] + face_z[:, :, 1:]
    return 1.0 / (scale * total)


def apply_operator(padded, coeffs, scale):
    face_x, face_y, face_z = coeffs
    centre = padded[1:-1, 1:-1, 1:-1]
    total = face_x[:-1] * (centre - padded[:-2, 1:-1, 1:-1]) + face_x[1:] * (centre - padded[2:, 1:-1, 1:-1])
    total = total + face_y[:, :-1] * (centre - padded[1:-1, :-2, 1:-1]) + face_y[:, 1:] * (centre - padded[1:-1, 2:, 1:-1])
    total = total + face_z[:, :, :-1] * (centre - padded[1:-1, 1:-1, :-2]) + face_z[:, :, 1:] * (centre - padded[1:-1, 1:-1, 2:])
    return scale * total


def jacobi_sweeps(field, source, coeffs, inverse, scale, count):
    for sweep_index in range(count):
        field = field + relax_weight * (source - apply_operator(pad_zeros(field), coeffs, scale)) * inverse
    return field


def conjugate_solve(source, coeffs, scale, count):
    field = jnp.zeros_like(source)
    remain = source
    direction = source
    norm_now = jnp.sum(remain * remain)
    for step_index in range(count):
        image = apply_operator(pad_zeros(direction), coeffs, scale)
        alpha = norm_now / jnp.sum(direction * image)
        field = field + alpha * direction
        remain = remain - alpha * image
        norm_next = jnp.sum(remain * remain)
        direction = remain + (norm_next / norm_now) * direction
        norm_now = norm_next
    return field


def restrict_mean(field):
    size_a, size_b, size_c = field.shape
    blocks = field.reshape(size_a // 2, 2, size_b // 2, 2, size_c // 2, 2)
    return jnp.mean(blocks, axis=(1, 3, 5))


def prolong_copy(field):
    return jnp.repeat(jnp.repeat(jnp.repeat(field, 2, axis=0), 2, axis=1), 2, axis=2)


def reference(right_side, beta):
    sources = [right_side]
    betas = [beta]
    saved = []
    for level in range(LEVELS):
        scale = 0.25 ** level
        coeffs = face_coeffs(pad_zeros(betas[level]))
        inverse = inverse_diagonal(coeffs, scale)
        field = jacobi_sweeps(jnp.zeros_like(sources[level]), sources[level], coeffs, inverse, scale, SWEEPS)
        residual = sources[level] - apply_operator(pad_zeros(field), coeffs, scale)
        saved.append((field, coeffs, inverse, scale))
        sources.append(restrict_mean(residual))
        betas.append(restrict_mean(betas[level]))
    low_scale = 0.25 ** LEVELS
    low_coeffs = face_coeffs(pad_zeros(betas[LEVELS]))
    field = conjugate_solve(sources[LEVELS], low_coeffs, low_scale, COARSE)
    for level in range(LEVELS - 1, -1, -1):
        kept, coeffs, inverse, scale = saved[level]
        field = kept + prolong_copy(field)
        field = jacobi_sweeps(field, sources[level], coeffs, inverse, scale, SWEEPS)
    return field
```

```python
import functools

import jax
import jax.numpy as jnp
from jax import lax
from jax.experimental import pallas as pl
from jax.experimental.pallas import tpu as pltpu
from jax.sharding import PartitionSpec as P

LEVELS = 4
SWEEPS = 2
COARSE = 8
W = 2.0 / 3.0
MESH = pl.DeviceIdType.MESH
F32 = jnp.float32

X0, Y0, LANES = 16, 32, 128
H0 = 4
H1 = 5
HY = 8
DIRS = [(dx, dy) for dx in (-1, 0, 1) for dy in (-1, 0, 1) if (dx, dy) != (0, 0)]


def roll(v, shift, axis):
    return pltpu.roll(v, shift % v.shape[axis], axis)


def lane_of(shape):
    return lax.broadcasted_iota(jnp.int32, shape, len(shape) - 1)


def pair_lanes(v, apart):
    lane = lane_of(v.shape)
    return v + jnp.where((lane & apart) == 0, roll(v, -apart, 1), roll(v, apart, 1))


def span(size, halo, step, near, far):
    if step == 0:
        return (halo, size), (halo, size)
    if step < 0:
        return (halo + near, far - near), (halo + size + near, far - near)
    return (halo + size - far, far - near), (halo - far, far - near)


def kernel(
    G, B, rs_ref, be_ref, out_ref,
    B0, S0, V0, U0, CX0, CY0, CM0, CP0, Q0, D0,
    B1, S1, V1, U1, CX1, CY1, CM1, CP1, Q1, D1,
    T, PB, PS, GB, GS, V2, C2, C3, C4, E, F3, LX0, LY0, LX1, LY1,
    halo_send, halo_recv, late_send, late_recv, ga_send, ga_recv, rounds, loc_sem,
):
    n = G * B
    g = lax.axis_index("grp")
    b = lax.axis_index("box")
    me = g * B + b
    ry2, ry3, ry4 = 8 * B, 4 * B, 2 * B

    own0 = (pl.ds(H0, X0), pl.ds(HY, Y0))
    load_b = pltpu.make_async_copy(be_ref, B0.at[own0[0], own0[1]], loc_sem.at[0])
    load_s = pltpu.make_async_copy(rs_ref, S0.at[own0[0], own0[1]], loc_sem.at[1])
    load_b.start()
    load_s.start()

    barrier = pltpu.get_barrier_semaphore()

    expected = 0
    for dx, dy in DIRS:
        there = (g + dx >= 0) & (g + dx < G) & (b + dy >= 0) & (b + dy < B)
        expected = expected + there.astype(jnp.int32)

        @pl.when(there)
        def _():
            pl.semaphore_signal(barrier, inc=1, device_id=(g + dx, b + dy), device_id_type=MESH)

    reach = max(1, -(-(B - 2) // 3))
    others = []
    for far in range(2, G):
        for dx in (-far, far):
            others += [(dx, dy) for dy in (-1, 0, 1)]
    for far in range(2, reach + 1):
        others += [(0, -far), (0, far)]
    for dx, dy in others:
        there = (g + dx >= 0) & (g + dx < G) & (b + dy >= 0) & (b + dy < B)
        expected = expected + there.astype(jnp.int32)

        @pl.when(there)
        def _():
            pl.semaphore_signal(barrier, inc=1, device_id=(g + dx, b + dy), device_id_type=MESH)

    def boxes_of(k):
        for far in range(k * reach + 1, (k + 1) * reach + 1):
            for dy in (-far, far):
                yield b + dy, (b + dy >= 0) & (b + dy < B)

    def tell(k):
        for other, there in boxes_of(k):

            @pl.when(there)
            def _():
                pl.semaphore_signal(rounds.at[k], inc=1, device_id=(g, other), device_id_type=MESH)

    def hear(k):
        count = 0
        for _, there in boxes_of(k):
            count = count + there.astype(jnp.int32)
        pl.semaphore_wait(rounds.at[k], count)

    for ref, nx, hx, ny in ((B0, X0, H0, Y0), (S0, X0, H0, Y0), (B1, X0 // 2, H1, Y0 // 2), (S1, X0 // 2, H1, Y0 // 2)):
        rows = ny + 2 * HY
        planes = nx + 2 * hx

        @pl.when(g == 0)
        def _():
            ref[pl.ds(0, hx)] = jnp.zeros((hx, rows, LANES), F32)

        @pl.when(g == G - 1)
        def _():
            ref[pl.ds(hx + nx, hx)] = jnp.zeros((hx, rows, LANES), F32)

        @pl.when(b == 0)
        def _():
            ref[:, pl.ds(0, HY)] = jnp.zeros((planes, HY, LANES), F32)

        @pl.when(b == B - 1)
        def _():
            ref[:, pl.ds(HY + ny, HY)] = jnp.zeros((planes, HY, LANES), F32)

    V2[0] = jnp.zeros((ry2 + 16, LANES), F32)
    V2[G + 1] = jnp.zeros((ry2 + 16, LANES), F32)
    V2[:, pl.ds(0, 8)] = jnp.zeros((G + 2, 8, LANES), F32)
    V2[:, pl.ds(8 + ry2, 8)] = jnp.zeros((G + 2, 8, LANES), F32)

    load_b.wait()

    def halve(pair, apart, slot):
        rows = pair.shape[0]
        T[slot, pl.ds(0, rows)] = pair_lanes(pair, apart)
        return 0.125 * (T[slot, pl.ds(0, rows // 2, stride=2)] + T[slot, pl.ds(1, rows // 2, stride=2)])

    def pack(planes):
        lane = lane_of(planes[0].shape) & 3
        packed = planes[3]
        for k in (2, 1, 0):
            packed = jnp.where(lane == k, planes[k], packed)
        return packed

    for p in range(X0 // 2):
        B1[H1 + p, pl.ds(HY, Y0 // 2)] = halve(
            B0[H0 + 2 * p, pl.ds(HY, Y0)] + B0[H0 + 2 * p + 1, pl.ds(HY, Y0)], 1, p
        )
    PB[...] = pack([
        halve(B1[H1 + 2 * p, pl.ds(HY, Y0 // 2)] + B1[H1 + 2 * p + 1, pl.ds(HY, Y0 // 2)], 2, p)
        for p in range(X0 // 4)
    ])

    load_s.wait()
    pl.semaphore_wait(barrier, expected)

    def there_from(dx, dy):
        return (g + dx >= 0) & (g + dx < G) & (b + dy >= 0) & (b + dy < B)

    def halo_copies(kind, ref, nx, hx, ny, deep, tall, corner):
        made = []
        for at, (dx, dy) in enumerate(DIRS):
            (sx, lx), (tx, _) = span(nx, hx, dx, 0, deep if dy == 0 else corner)
            (sy, ly), (ty, _) = span(ny, HY, dy, 0, tall if dx == 0 else corner)
            copy = pltpu.make_async_remote_copy(
                src_ref=ref.at[pl.ds(sx, lx), pl.ds(sy, ly)],
                dst_ref=ref.at[pl.ds(tx, lx), pl.ds(ty, ly)],
                send_sem=halo_send.at[kind, at],
                recv_sem=halo_recv.at[kind, at],
                device_id=(g + dx, b + dy),
                device_id_type=MESH,
            )
            made.append((copy, there_from(dx, dy), there_from(-dx, -dy)))
        return made

    def late_copies(kind, ref, LX, LY, nx, hx, ny, near, far):
        made, land = [], []
        for at, (dx, dy) in enumerate(((-1, 0), (1, 0), (0, -1), (0, 1))):
            (sx, lx), (tx, _) = span(nx, hx, dx, near, far)
            (sy, ly), (ty, _) = span(ny, HY, dy, near, far)
            box = LX.at[at] if dy == 0 else LY.at[at - 2, :, pl.ds(0, far - near)]
            copy = pltpu.make_async_remote_copy(
                src_ref=ref.at[pl.ds(sx, lx), pl.ds(sy, ly)],
                dst_ref=box,
                send_sem=late_send.at[kind, at],
                recv_sem=late_recv.at[kind, at],
                device_id=(g + dx, b + dy),
                device_id_type=MESH,
            )
            here = there_from(-dx, -dy)
            made.append((copy, there_from(dx, dy), here))

            def put(tx=tx, lx=lx, ty=ty, ly=ly, box=box):
                ref[pl.ds(tx, lx), pl.ds(ty, ly)] = box[...]

            land.append((here, put))
        return made, land

    def land_all(late):
        made, land = late
        for (copy, _, here), (_, put) in zip(made, land):

            @pl.when(here)
            def _():
                copy.wait_recv()
                put()

    def start_all(copies):
        for copy, there, _ in copies:
            pl.when(there)(copy.start)

    def recv_all(copies):
        for copy, _, here in copies:
            pl.when(here)(copy.wait_recv)

    def sent_all(copies):
        for copy, there, _ in copies:
            pl.when(there)(copy.wait_send)

    def gather_start(which, packed, whole):
        pltpu.make_async_copy(packed, whole.at[g, pl.ds(pl.multiple_of(b * 8, 8), 8)], ga_recv.at[which]).start()

        def one(d, carry):
            peer = (me + d) % n
            pltpu.make_async_remote_copy(
                src_ref=packed,
                dst_ref=whole.at[g, pl.ds(pl.multiple_of(b * 8, 8), 8)],
                send_sem=ga_send.at[which, d],
                recv_sem=ga_recv.at[which],
                device_id=(peer // B, peer % B),
                device_id_type=MESH,
            ).start()
            return carry

        lax.fori_loop(1, n, one, 0, unroll=True)

    def gather_recv(which, whole):
        pltpu.make_async_copy(whole, whole, ga_recv.at[which]).wait()

    def gather_sent(which, packed):
        def one(d, carry):
            pltpu.make_async_copy(packed, packed, ga_send.at[which, d]).wait()
            return carry

        lax.fori_loop(1, n, one, 0, unroll=True)

    beta_halo = halo_copies(0, B0, X0, H0, Y0, 3, 3, 3)
    source_halo = halo_copies(1, S0, X0, H0, Y0, 2, 2, 2)
    beta1_halo = halo_copies(2, B1, X0 // 2, H1, Y0 // 2, 5, 5, 5)
    beta_late = late_copies(0, B0, LX0.at[0], LY0.at[0], X0, H0, Y0, 3, 4)
    source_late = late_copies(1, S0, LX0.at[1], LY0.at[1], X0, H0, Y0, 2, 3)
    start_all(beta_halo)
    start_all(source_halo)
    tell(0)
    start_all(beta1_halo)

    def setup(level, Bl, CX, CY, CM, CP, Q, D, first, last, row, rows, hx, nx, ny):
        apart = 1 << level
        h = 0.5 * 0.25**level

        def plane(i, carry):
            at = pl.ds(row, rows)
            c = Bl[i, at]
            xm = Bl[i - 1, at]
            xp = Bl[i + 1, at]
            ym = Bl[i, pl.ds(row - 1, rows)]
            yp = Bl[i, pl.ds(row + 1, rows)]
            lane = lane_of(c.shape)
            low = lane >= apart
            high = lane < LANES - apart
            zm = jnp.where(low, roll(c, apart, 1), 0.0)
            zp = jnp.where(high, roll(c, -apart, 1), 0.0)
            CX[i, at] = h * (c + xm)
            CY[i, at] = h * (c + ym)
            CM[i, at] = jnp.where(low, h * (c + zm), 0.0)
            CP[i, at] = jnp.where(high, h * (c + zp), 0.0)
            d = h * (6.0 * c + ((xm + xp) + (ym + yp) + (zm + zp)))
            D[i, at] = d
            x = g * nx + i - hx
            y = lax.broadcasted_iota(jnp.int32, c.shape, 0) + (b * ny + row - HY)
            inside = (y >= 0) & (y < B * ny) & (x >= 0) & (x < G * nx)
            Q[i, at] = jnp.where(inside, W / d, 0.0)
            return carry

        lax.fori_loop(first, last, plane, 0, unroll=True)

    def across(level, V, CX, CY, CM, CP, i, row, rows):
        apart = 1 << level
        at = pl.ds(row, rows)
        up = pl.ds(row + 1, rows)
        v = V[i, at]
        total = CX[i, at] * V[i - 1, at] + CX[i + 1, at] * V[i + 1, at]
        total = total + (CY[i, at] * V[i, pl.ds(row - 1, rows)] + CY[i, up] * V[i, up])
        total = total + (CM[i, at] * roll(v, apart, 1) + CP[i, at] * roll(v, -apart, 1))
        return v, total

    def first_sweep(V, Q, S, first, last, row, rows):
        def plane(i, carry):
            V[i, pl.ds(row, rows)] = Q[i, pl.ds(row, rows)] * S[i, pl.ds(row, rows)]
            return carry

        lax.fori_loop(first, last, plane, 0, unroll=True)

    def sweep(level, V, U, S, Q, coeffs, first, last, row, rows, drop_x=0, drop_y=0):
        def plane(i, carry):
            v, total = across(level, V, *coeffs, i, row, rows)
            U[i - drop_x, pl.ds(row - drop_y, rows)] = (1.0 - W) * v + Q[i, pl.ds(row, rows)] * (
                S[i, pl.ds(row, rows)] + total
            )
            return carry

        lax.fori_loop(first, last, plane, 0, unroll=True)

    def residual(level, V, S, D, coeffs, i, row, rows):
        v, total = across(level, V, *coeffs, i, row, rows)
        return S[i, pl.ds(row, rows)] - (D[i, pl.ds(row, rows)] * v - total)

    coeffs0 = (CX0, CY0, CM0, CP0)
    coeffs1 = (CX1, CY1, CM1, CP1)
    row0, rows0 = 4, 40
    row1, rows1 = 4, 24

    recv_all(beta_halo)
    hear(0)
    tell(1)
    setup(0, B0, CX0, CY0, CM0, CP0, Q0, D0, 2, 22, row0, rows0, H0, X0, Y0)
    recv_all(source_halo)
    first_sweep(V0, Q0, S0, 2, 22, row0, rows0)
    sweep(0, V0, U0, S0, Q0, coeffs0, 3, 21, row0, rows0)

    def down0(p, carry):
        i = H0 + 2 * p
        pair = residual(0, U0, S0, D0, coeffs0, i, HY, Y0) + residual(0, U0, S0, D0, coeffs0, i + 1, HY, Y0)
        S1[H1 + p, pl.ds(HY, Y0 // 2)] = halve(pair, 1, p)
        return carry

    lax.fori_loop(0, X0 // 2, down0, 0, unroll=True)
    source1_halo = halo_copies(3, S1, X0 // 2, H1, Y0 // 2, 2, 2, 4)
    source1_late = late_copies(2, S1, LX1, LY1, X0 // 2, H1, Y0 // 2, 2, 4)
    start_all(source1_halo)
    hear(1)
    gather_start(0, PB, GB)
    start_all(source1_late[0])
    start_all(beta_late[0])
    start_all(source_late[0])

    recv_all(beta1_halo)
    setup(1, B1, CX1, CY1, CM1, CP1, Q1, D1, 1, 17, row1, rows1, H1, X0 // 2, Y0 // 2)
    recv_all(source1_halo)
    first_sweep(V1, Q1, S1, 3, 15, row1, rows1)
    sweep(1, V1, U1, S1, Q1, coeffs1, 4, 14, row1, rows1)
    planes = []
    for p in range(X0 // 4):
        i = H1 + 2 * p
        pair = residual(1, U1, S1, D1, coeffs1, i, HY, Y0 // 2) + residual(1, U1, S1, D1, coeffs1, i + 1, HY, Y0 // 2)
        planes.append(halve(pair, 2, p))
    PS[...] = pack(planes)
    gather_start(1, PS, GS)

    land_all(source1_late)
    first_sweep(V1, Q1, S1, 1, 17, row1, rows1)
    sweep(1, V1, U1, S1, Q1, coeffs1, 2, 16, row1, rows1)
    land_all(beta_late)
    land_all(source_late)
    setup(0, B0, CX0, CY0, CM0, CP0, Q0, D0, 1, 23, row0, rows0, H0, X0, Y0)
    first_sweep(V0, Q0, S0, 1, 23, row0, rows0)
    sweep(0, V0, U0, S0, Q0, coeffs0, 2, 22, row0, rows0)

    def neighbours(v, level):
        st, zs = 1 << (level - 2), 1 << level
        before = [v[i - 1] for i in range(G)]
        after = [v[(i + 1) % G] for i in range(G)]
        if st == 4:
            xm, xp = before, after
        else:
            k = lane_of(v[0].shape) & 3
            xm = [jnp.where(k >= st, roll(v[i], st, 1), roll(before[i], st - 4, 1)) for i in range(G)]
            xp = [jnp.where(k < 4 - st, roll(v[i], -st, 1), roll(after[i], 4 - st, 1)) for i in range(G)]
        ym = [roll(a, 1, 0) for a in v]
        yp = [roll(a, -1, 0) for a in v]
        zm = [roll(a, zs, 1) for a in v]
        zp = [roll(a, -zs, 1) for a in v]
        return xm, xp, ym, yp, zm, zp

    def setup_whole(beta, C, level):
        st, zs = 1 << (level - 2), 1 << level
        h = 0.5 * 0.25**level
        near = neighbours(beta, level)
        shape = beta[0].shape
        lane = lane_of(shape)
        row = lax.broadcasted_iota(jnp.int32, shape, 0)
        for i in range(G):
            ok = [
                ((lane & 3) >= st) if i == 0 else None,
                ((lane & 3) < 4 - st) if i == G - 1 else None,
                row > 0,
                row < shape[0] - 1,
                lane >= zs,
                lane < LANES - zs,
            ]
            total = 6.0 * beta[i]
            for d in range(6):
                there = near[d][i] if ok[d] is None else jnp.where(ok[d], near[d][i], 0.0)
                total = total + there
                face = h * (beta[i] + there)
                C[d, i] = face if ok[d] is None else jnp.where(ok[d], face, 0.0)
            diag = h * total
            C[6, i] = diag
            C[7, i] = W / diag

    def sum_across(v, C, level):
        near = neighbours(v, level)
        out = []
        for i in range(G):
            out.append(
                (C[0, i] * near[0][i] + C[1, i] * near[1][i])
                + (C[2, i] * near[2][i] + C[3, i] * near[3][i])
                + (C[4, i] * near[4][i] + C[5, i] * near[5][i])
            )
        return out

    def sweep_whole(v, s, C, level):
        total = sum_across(v, C, level)
        return [(1.0 - W) * v[i] + C[7, i] * (s[i] + total[i]) for i in range(G)]

    def coarsen(v, level):
        st, zs = 1 << (level - 2), 1 << level
        rows = v[0].shape[0]
        out = []
        for i in range(G):
            E[i, pl.ds(0, rows)] = pair_lanes(pair_lanes(v[i], st), zs)
            out.append(0.125 * (E[i, pl.ds(0, rows // 2, stride=2)] + E[i, pl.ds(1, rows // 2, stride=2)]))
        return out

    def refine(v):
        rows = v[0].shape[0]
        out = []
        for i in range(G):
            E[i, pl.ds(0, rows, stride=2)] = v[i]
            E[i, pl.ds(1, rows, stride=2)] = v[i]
            out.append(E[i, pl.ds(0, 2 * rows)])
        return out

    gather_recv(0, GB)
    beta2 = [GB[i] for i in range(G)]
    setup_whole(beta2, C2, 2)
    beta3 = coarsen(beta2, 2)
    setup_whole(beta3, C3, 3)
    beta4 = coarsen(beta3, 3)
    setup_whole(beta4, C4, 4)

    gather_recv(1, GS)
    s2 = [GS[i] for i in range(G)]
    v = [C2[7, i] * s2[i] for i in range(G)]
    v = sweep_whole(v, s2, C2, 2)
    for i in range(G):
        V2[i + 1, pl.ds(8, ry2)] = v[i]
    total = sum_across(v, C2, 2)
    s3 = coarsen([s2[i] - (C2[6, i] * v[i] - total[i]) for i in range(G)], 2)
    v = [C3[7, i] * s3[i] for i in range(G)]
    v = sweep_whole(v, s3, C3, 3)
    for i in range(G):
        F3[0, i] = v[i]
        F3[1, i] = s3[i]
    total = sum_across(v, C3, 3)
    s4 = coarsen([s3[i] - (C3[6, i] * v[i] - total[i]) for i in range(G)], 3)

    def dot(a, c):
        acc = a[0] * c[0]
        for i in range(1, G):
            acc = acc + a[i] * c[i]
        part = acc[0:8]
        for j in range(8, ry4, 8):
            part = part + acc[j : j + 8]
        return jnp.sum(jnp.sum(part, axis=0, keepdims=True), axis=1, keepdims=True)

    def cg(step, carry):
        x, r, p, rr = carry
        near = sum_across(p, C4, 4)
        q = [C4[6, i] * p[i] - near[i] for i in range(G)]
        alpha = rr / dot(p, q)
        x = [x[i] + alpha * p[i] for i in range(G)]
        r = [r[i] - alpha * q[i] for i in range(G)]
        new = dot(r, r)
        ratio = new / rr
        p = [r[i] + ratio * p[i] for i in range(G)]
        return x, r, p, new

    zero = [jnp.zeros((ry4, LANES), F32) for i in range(G)]
    x4 = lax.fori_loop(0, COARSE, cg, (zero, s4, s4, dot(s4, s4)), unroll=True)[0]

    up = refine(x4)
    s3 = [F3[1, i] for i in range(G)]
    v = [F3[0, i] + up[i] for i in range(G)]
    for _ in range(SWEEPS):
        v = sweep_whole(v, s3, C3, 3)
    up = refine(v)
    s2 = [GS[i] for i in range(G)]
    v = [V2[i + 1, pl.ds(8, ry2)] + up[i] for i in range(G)]
    for _ in range(SWEEPS):
        v = sweep_whole(v, s2, C2, 2)
    for i in range(G):
        V2[i + 1, pl.ds(8, ry2)] = v[i]

    for x2 in range(-2, 6):
        k = x2 % 4
        window = V2[g + 1 + x2 // 4, pl.ds(pl.multiple_of(b * 8, 8), 24)]
        one = jnp.where((lane_of(window.shape) & 3) == k, window, 0.0)
        one = one + roll(one, 1 if k in (0, 2) else -1, 1)
        one = one + roll(one, 2 if k in (0, 1) else -2, 1)
        T[x2 + 2, pl.ds(0, 24)] = one
    for x2 in range(-2, 6):
        add = T[x2 + 2, pl.ds(6, 12)]
        for i in (2 * x2 + 5, 2 * x2 + 6):
            if 2 <= i < 16:
                for odd in (0, 1):
                    at = pl.ds(row1 + odd, 12, stride=2)
                    U1[i, at] = U1[i, at] + add
    sweep(1, U1, V1, S1, Q1, coeffs1, 3, 15, row1, rows1)
    sweep(1, V1, U1, S1, Q1, coeffs1, 4, 14, row1, rows1)

    def prolong0(i, carry):
        add = U1[i + 3, pl.ds(6, 20)]
        for half in (0, 1):
            for odd in (0, 1):
                at = pl.ds(row0 + odd, 20, stride=2)
                U0[2 * i + half, at] = U0[2 * i + half, at] + add
        return carry

    lax.fori_loop(1, 11, prolong0, 0, unroll=True)
    sweep(0, U0, V0, S0, Q0, coeffs0, 3, 21, row0, rows0)
    sweep(0, V0, out_ref, S0, Q0, coeffs0, 4, 20, HY, Y0, H0, HY)

    sent_all(beta_halo)
    sent_all(source_halo)
    sent_all(beta1_halo)
    sent_all(source1_halo)
    sent_all(beta_late[0])
    sent_all(source_late[0])
    sent_all(source1_late[0])
    gather_sent(0, PB)
    gather_sent(1, PS)


def in_one_kernel(G, B, right_side, beta):
    level0 = pltpu.VMEM((X0 + 2 * H0, Y0 + 2 * HY, LANES), F32)
    level1 = pltpu.VMEM((X0 // 2 + 2 * H1, Y0 // 2 + 2 * HY, LANES), F32)
    return pl.pallas_call(
        functools.partial(kernel, G, B),
        out_shape=jax.ShapeDtypeStruct(right_side.shape, F32),
        in_specs=[pl.BlockSpec(memory_space=pltpu.HBM)] * 2,
        out_specs=pl.BlockSpec(memory_space=pltpu.VMEM),
        scratch_shapes=[level0] * 10
        + [level1] * 10
        + [
            pltpu.VMEM((8, Y0, LANES), F32),
            pltpu.VMEM((8, LANES), F32),
            pltpu.VMEM((8, LANES), F32),
            pltpu.VMEM((G, 8 * B, LANES), F32),
            pltpu.VMEM((G, 8 * B, LANES), F32),
            pltpu.VMEM((G + 2, 8 * B + 16, LANES), F32),
            pltpu.VMEM((8, G, 8 * B, LANES), F32),
            pltpu.VMEM((8, G, 4 * B, LANES), F32),
            pltpu.VMEM((8, G, 2 * B, LANES), F32),
            pltpu.VMEM((G, 8 * B, LANES), F32),
            pltpu.VMEM((2, G, 4 * B, LANES), F32),
            pltpu.VMEM((2, 2, 1, Y0, LANES), F32),
            pltpu.VMEM((2, 2, X0, 8, LANES), F32),
            pltpu.VMEM((2, 2, Y0 // 2, LANES), F32),
            pltpu.VMEM((2, X0 // 2, 8, LANES), F32),
            pltpu.SemaphoreType.DMA((4, 8)),
            pltpu.SemaphoreType.DMA((4, 8)),
            pltpu.SemaphoreType.DMA((3, 4)),
            pltpu.SemaphoreType.DMA((3, 4)),
            pltpu.SemaphoreType.DMA((2, G * B)),
            pltpu.SemaphoreType.DMA((2,)),
            pltpu.SemaphoreType.REGULAR((8,)),
            pltpu.SemaphoreType.DMA((2,)),
        ],
        compiler_params=pltpu.CompilerParams(
            collective_id=0, has_side_effects=True, vmem_limit_bytes=40 * 1024 * 1024
        ),
    )(*(pltpu.with_memory_space_constraint(a, pltpu.HBM) for a in (right_side, beta)))


relax_weight = 2.0 / 3.0


def with_halo(shard, sides, width):
    for axis, dim in sides:
        size, length = (lax.axis_size(axis), shard.shape[dim])
        up = [(i, (i + 1) % size) for i in range(size - 1)]
        down = [(j, i) for i, j in up]
        last = lax.slice_in_dim(shard, length - width, length, axis=dim)
        leading = lax.slice_in_dim(shard, 0, width, axis=dim)
        before = lax.ppermute(last, axis, up)
        after = lax.ppermute(leading, axis, down)
        shard = jnp.concatenate([before, shard, after], axis=dim)
    return shard


def from_partner(block, axis, apart):
    count = lax.axis_size(axis)
    route = []
    for low in range(count):
        high = low | 1 << apart
        if high != low and high < count:
            route += [(low, high), (high, low)]
    return lax.ppermute(block, axis, route)


def pad_zeros(field):
    return jnp.pad(field, 1)


def pad_local(field):
    extended = with_halo(field, (("grp", 0), ("box", 1)), 1)
    return jnp.pad(extended, ((0, 0), (0, 0), (1, 1)))


def face_coeffs(padded_beta):
    face_x = 0.5 * (padded_beta[1:, 1:-1, 1:-1] + padded_beta[:-1, 1:-1, 1:-1])
    face_y = 0.5 * (padded_beta[1:-1, 1:, 1:-1] + padded_beta[1:-1, :-1, 1:-1])
    face_z = 0.5 * (padded_beta[1:-1, 1:-1, 1:] + padded_beta[1:-1, 1:-1, :-1])
    return (face_x, face_y, face_z)


def inverse_diagonal(coeffs, scale):
    face_x, face_y, face_z = coeffs
    total = (
        face_x[:-1]
        + face_x[1:]
        + face_y[:, :-1]
        + face_y[:, 1:]
        + face_z[:, :, :-1]
        + face_z[:, :, 1:]
    )
    return 1.0 / (scale * total)


def apply_operator(padded, coeffs, scale):
    face_x, face_y, face_z = coeffs
    centre = padded[1:-1, 1:-1, 1:-1]
    total = face_x[:-1] * (centre - padded[:-2, 1:-1, 1:-1]) + face_x[1:] * (
        centre - padded[2:, 1:-1, 1:-1]
    )
    total = (
        total
        + face_y[:, :-1] * (centre - padded[1:-1, :-2, 1:-1])
        + face_y[:, 1:] * (centre - padded[1:-1, 2:, 1:-1])
    )
    total = (
        total
        + face_z[:, :, :-1] * (centre - padded[1:-1, 1:-1, :-2])
        + face_z[:, :, 1:] * (centre - padded[1:-1, 1:-1, 2:])
    )
    return scale * total


def jacobi_sweeps(field, source, coeffs, inverse, scale, count, padder):
    for sweep_index in range(count):
        field = (
            field + relax_weight * (source - apply_operator(padder(field), coeffs, scale)) * inverse
        )
    return field


def conjugate_solve(source, coeffs, scale, count):
    field = jnp.zeros_like(source)
    remain = source
    direction = source
    norm_now = jnp.sum(remain * remain)
    for step_index in range(count):
        image = apply_operator(pad_zeros(direction), coeffs, scale)
        alpha = norm_now / jnp.sum(direction * image)
        field = field + alpha * direction
        remain = remain - alpha * image
        norm_next = jnp.sum(remain * remain)
        direction = remain + norm_next / norm_now * direction
        norm_now = norm_next
    return field


def restrict_mean(field):
    size_a, size_b, size_c = field.shape
    blocks = field.reshape(size_a // 2, 2, size_b // 2, 2, size_c // 2, 2)
    return jnp.mean(blocks, axis=(1, 3, 5))


def prolong_copy(field):
    return jnp.repeat(jnp.repeat(jnp.repeat(field, 2, axis=0), 2, axis=1), 2, axis=2)


def merge_groups(pieces):
    group_index = lax.axis_index("grp")
    for bit_index in range(lax.axis_size("grp").bit_length() - 1):
        partner = from_partner(pieces, "grp", bit_index)
        upper = group_index >> bit_index & 1 == 1
        pieces = tuple(
            (
                jnp.where(
                    upper,
                    jnp.concatenate([theirs, own_piece], 0),
                    jnp.concatenate([own_piece, theirs], 0),
                )
                for own_piece, theirs in zip(pieces, partner)
            )
        )
    return pieces


def merge_boxes(pieces):
    return lax.all_gather(pieces, "box", axis=1, tiled=True)


def shards(right_side, beta):
    source = right_side
    level_beta = beta
    saved = []
    for level in range(LEVELS):
        scale = 0.25**level
        coeffs = face_coeffs(pad_local(level_beta))
        inverse = inverse_diagonal(coeffs, scale)
        field = relax_weight * source * inverse
        field = jacobi_sweeps(field, source, coeffs, inverse, scale, SWEEPS - 1, pad_local)
        residual = source - apply_operator(pad_local(field), coeffs, scale)
        saved.append((field, source, coeffs, inverse, scale))
        source = restrict_mean(residual)
        level_beta = restrict_mean(level_beta)
    low_scale = 0.25**LEVELS
    whole_source, whole_beta = merge_boxes(merge_groups((source, level_beta)))
    low_coeffs = face_coeffs(pad_zeros(whole_beta))
    whole_field = conjugate_solve(whole_source, low_coeffs, low_scale, COARSE)
    block_a, block_b, block_c = source.shape
    field = lax.dynamic_slice(
        whole_field,
        (lax.axis_index("grp") * block_a, lax.axis_index("box") * block_b, 0),
        (block_a, block_b, block_c),
    )
    for level in range(LEVELS - 1, -1, -1):
        kept, level_source, coeffs, inverse, scale = saved[level]
        field = kept + prolong_copy(field)
        field = jacobi_sweeps(field, level_source, coeffs, inverse, scale, SWEEPS, pad_local)
    return field


def solution(mesh):
    placed = P("grp", "box", None)
    G, B = mesh.shape["grp"], mesh.shape["box"]
    small = (G, B) in ((4, 8), (8, 8), (4, 16), (8, 4), (2, 16))

    def local(right_side, beta):
        if small and right_side.shape == (X0, Y0, LANES):
            return in_one_kernel(G, B, right_side, beta)
        return shards(right_side, beta)

    return jax.shard_map(local, mesh=mesh, in_specs=(placed, placed), out_specs=placed, check_vma=False)
```

```python
import functools

import jax
import jax.numpy as jnp
from jax import lax
from jax.experimental import pallas as pl
from jax.experimental.pallas import tpu as pltpu
from jax.sharding import PartitionSpec as P

LEVELS = 4
SWEEPS = 2
COARSE = 8
W = 2.0 / 3.0
MESH = pl.DeviceIdType.MESH
F32 = jnp.float32

X0, Y0, LANES = 16, 32, 128
H0 = 4
H1 = 5
HY = 8
DIRS = [(dx, dy) for dx in (-1, 0, 1) for dy in (-1, 0, 1) if (dx, dy) != (0, 0)]


def roll(v, shift, axis):
    return pltpu.roll(v, shift % v.shape[axis], axis)


def lane_of(shape):
    return lax.broadcasted_iota(jnp.int32, shape, len(shape) - 1)


def pair_lanes(v, apart):
    lane = lane_of(v.shape)
    return v + jnp.where((lane & apart) == 0, roll(v, -apart, 1), roll(v, apart, 1))


def span(size, halo, step, near, far):
    if step == 0:
        return (halo, size), (halo, size)
    if step < 0:
        return (halo + near, far - near), (halo + size + near, far - near)
    return (halo + size - far, far - near), (halo - far, far - near)


def kernel(
    G, B, rs_ref, be_ref, out_ref,
    B0, S0, V0, U0, CX0, CY0, CM0, CP0, Q0, D0,
    B1, S1, V1, U1, CX1, CY1, CM1, CP1, Q1, D1,
    T, SZ1, PB, PS, P3, PG, GB, GS, GE, V2, Z2, C2, C3, C4, E, E2, F, F3, LX0, LY0, LX1, LY1,
    halo_send, halo_recv, late_send, late_recv, win_send, win_recv, ga_send, ga_recv, rounds, loc_sem,
):
    n = G * B
    g = lax.axis_index("grp")
    b = lax.axis_index("box")
    me = g * B + b
    ry2, ry3, ry4 = 8 * B, 4 * B, 2 * B

    own0 = (pl.ds(H0, X0), pl.ds(HY, Y0))
    load_b = pltpu.make_async_copy(be_ref, B0.at[own0[0], own0[1]], loc_sem.at[0])
    load_s = pltpu.make_async_copy(rs_ref, S0.at[own0[0], own0[1]], loc_sem.at[1])
    load_b.start()
    load_s.start()

    barrier = pltpu.get_barrier_semaphore()

    expected = 0
    for dx, dy in DIRS:
        there = (g + dx >= 0) & (g + dx < G) & (b + dy >= 0) & (b + dy < B)
        expected = expected + there.astype(jnp.int32)

        @pl.when(there)
        def _():
            pl.semaphore_signal(barrier, inc=1, device_id=(g + dx, b + dy), device_id_type=MESH)

    reach = max(1, -(-(B - 2) // 3))
    others = []
    for far in range(2, G):
        for dx in (-far, far):
            others += [(dx, dy) for dy in (-1, 0, 1)]
    for far in range(2, reach + 1):
        others += [(0, -far), (0, far)]
    for dx, dy in others:
        there = (g + dx >= 0) & (g + dx < G) & (b + dy >= 0) & (b + dy < B)
        expected = expected + there.astype(jnp.int32)

        @pl.when(there)
        def _():
            pl.semaphore_signal(barrier, inc=1, device_id=(g + dx, b + dy), device_id_type=MESH)

    def boxes_of(k):
        for far in range(k * reach + 1, (k + 1) * reach + 1):
            for dy in (-far, far):
                yield b + dy, (b + dy >= 0) & (b + dy < B)

    def tell(k):
        for other, there in boxes_of(k):

            @pl.when(there)
            def _():
                pl.semaphore_signal(rounds.at[k], inc=1, device_id=(g, other), device_id_type=MESH)

    def hear(k):
        count = 0
        for _, there in boxes_of(k):
            count = count + there.astype(jnp.int32)
        pl.semaphore_wait(rounds.at[k], count)

    for ref, nx, hx, ny in ((B0, X0, H0, Y0), (S0, X0, H0, Y0), (B1, X0 // 2, H1, Y0 // 2), (S1, X0 // 2, H1, Y0 // 2)):
        rows = ny + 2 * HY
        planes = nx + 2 * hx

        @pl.when(g == 0)
        def _():
            ref[pl.ds(0, hx)] = jnp.zeros((hx, rows, LANES), F32)

        @pl.when(g == G - 1)
        def _():
            ref[pl.ds(hx + nx, hx)] = jnp.zeros((hx, rows, LANES), F32)

        @pl.when(b == 0)
        def _():
            ref[:, pl.ds(0, HY)] = jnp.zeros((planes, HY, LANES), F32)

        @pl.when(b == B - 1)
        def _():
            ref[:, pl.ds(HY + ny, HY)] = jnp.zeros((planes, HY, LANES), F32)

    for ref in (SZ1, V1, U1, V2, Z2):
        ref[...] = jnp.zeros(ref.shape, F32)
    for side, edge in ((0, 0), (16, B - 1)):
        for ref in (GB, GS):

            @pl.when(b == edge)
            def _():
                ref[:, pl.ds(side, 8)] = jnp.zeros((G, 8, LANES), F32)

    E2[:, pl.ds(0, 8)] = jnp.zeros((G, 8, LANES), F32)
    E2[:, pl.ds(8 + ry2, 8)] = jnp.zeros((G, 8, LANES), F32)
    F[0] = jnp.zeros((8, LANES), F32)
    F[G + 1] = jnp.zeros((8, LANES), F32)
    GE[:, :, pl.ds(0, 8)] = jnp.zeros((2, G, 8, LANES), F32)
    GE[:, :, pl.ds(8 + ry3, 8)] = jnp.zeros((2, G, 8, LANES), F32)

    load_b.wait()

    def halve(pair, apart, slot):
        rows = pair.shape[0]
        T[slot, pl.ds(0, rows)] = pair_lanes(pair, apart)
        return 0.125 * (T[slot, pl.ds(0, rows // 2, stride=2)] + T[slot, pl.ds(1, rows // 2, stride=2)])

    def pack(planes):
        lane = lane_of(planes[0].shape) & 3
        packed = planes[3]
        for k in (2, 1, 0):
            packed = jnp.where(lane == k, planes[k], packed)
        return packed

    for p in range(X0 // 2):
        B1[H1 + p, pl.ds(HY, Y0 // 2)] = halve(
            B0[H0 + 2 * p, pl.ds(HY, Y0)] + B0[H0 + 2 * p + 1, pl.ds(HY, Y0)], 1, p
        )
    PB[...] = pack([
        halve(B1[H1 + 2 * p, pl.ds(HY, Y0 // 2)] + B1[H1 + 2 * p + 1, pl.ds(HY, Y0 // 2)], 2, p)
        for p in range(X0 // 4)
    ])
    GB[g, pl.ds(8, 8)] = PB[...]
    T[0, pl.ds(0, 8)] = pair_lanes(pair_lanes(PB[...], 1), 4)
    P3[...] = jnp.zeros((8, LANES), F32)
    P3[pl.ds(2, 4)] = 0.125 * (T[0, pl.ds(0, 4, stride=2)] + T[0, pl.ds(1, 4, stride=2)])

    load_s.wait()
    pl.semaphore_wait(barrier, expected)

    def there_from(dx, dy):
        return (g + dx >= 0) & (g + dx < G) & (b + dy >= 0) & (b + dy < B)

    def halo_copies(kind, ref, nx, hx, ny, deep, tall, corner):
        made = []
        for at, (dx, dy) in enumerate(DIRS):
            (sx, lx), (tx, _) = span(nx, hx, dx, 0, deep if dy == 0 else corner)
            (sy, ly), (ty, _) = span(ny, HY, dy, 0, tall if dx == 0 else corner)
            copy = pltpu.make_async_remote_copy(
                src_ref=ref.at[pl.ds(sx, lx), pl.ds(sy, ly)],
                dst_ref=ref.at[pl.ds(tx, lx), pl.ds(ty, ly)],
                send_sem=halo_send.at[kind, at],
                recv_sem=halo_recv.at[kind, at],
                device_id=(g + dx, b + dy),
                device_id_type=MESH,
            )
            made.append((copy, there_from(dx, dy), there_from(-dx, -dy)))
        return made

    def late_copies(kind, ref, LX, LY, nx, hx, ny, near, far):
        made, land = [], []
        for at, (dx, dy) in enumerate(((-1, 0), (1, 0), (0, -1), (0, 1))):
            (sx, lx), (tx, _) = span(nx, hx, dx, near, far)
            (sy, ly), (ty, _) = span(ny, HY, dy, near, far)
            box = LX.at[at] if dy == 0 else LY.at[at - 2, :, pl.ds(0, far - near)]
            copy = pltpu.make_async_remote_copy(
                src_ref=ref.at[pl.ds(sx, lx), pl.ds(sy, ly)],
                dst_ref=box,
                send_sem=late_send.at[kind, at],
                recv_sem=late_recv.at[kind, at],
                device_id=(g + dx, b + dy),
                device_id_type=MESH,
            )
            here = there_from(-dx, -dy)
            made.append((copy, there_from(dx, dy), here))

            def put(tx=tx, lx=lx, ty=ty, ly=ly, box=box):
                ref[pl.ds(tx, lx), pl.ds(ty, ly)] = box[...]

            land.append((here, put))
        return made, land

    def land_all(late):
        made, land = late
        for (copy, _, here), (_, put) in zip(made, land):

            @pl.when(here)
            def _():
                copy.wait_recv()
                put()

    def start_all(copies):
        for copy, there, _ in copies:
            pl.when(there)(copy.start)

    def recv_all(copies):
        for copy, _, here in copies:
            pl.when(here)(copy.wait_recv)

    def sent_all(copies):
        for copy, there, _ in copies:
            pl.when(there)(copy.wait_send)

    def window_copies(kind, packed, whole):
        made = []
        for o in range(G):
            for dy in (-1, 0, 1):
                if (o, dy) == (0, 0):
                    continue
                at = 3 * o + dy + 1
                copy = pltpu.make_async_remote_copy(
                    src_ref=packed,
                    dst_ref=whole.at[g, pl.ds(8 - 8 * dy, 8)],
                    send_sem=win_send.at[kind, at],
                    recv_sem=win_recv.at[kind, at],
                    device_id=((g + o) % G, b + dy),
                    device_id_type=MESH,
                )
                made.append((copy, (b + dy >= 0) & (b + dy < B), (b - dy >= 0) & (b - dy < B)))
        return made

    def gather_start():
        spot = GE.at[b % 2, g, pl.ds(pl.multiple_of(8 + 8 * (b // 2), 8), 8)]
        pltpu.make_async_copy(PG, spot, ga_recv.at[0]).start()

        def one(d, carry):
            peer = (me + d) % n
            pltpu.make_async_remote_copy(
                src_ref=PG,
                dst_ref=spot,
                send_sem=ga_send.at[d],
                recv_sem=ga_recv.at[0],
                device_id=(peer // B, peer % B),
                device_id_type=MESH,
            ).start()
            return carry

        lax.fori_loop(1, n, one, 0, unroll=True)

    def gather_recv():
        whole = GE.at[:, :, pl.ds(8, ry3)]
        pltpu.make_async_copy(whole, whole, ga_recv.at[0]).wait()

    def gather_sent():
        def one(d, carry):
            pltpu.make_async_copy(PG, PG, ga_send.at[d]).wait()
            return carry

        lax.fori_loop(1, n, one, 0, unroll=True)

    beta_halo = halo_copies(0, B0, X0, H0, Y0, 3, 3, 3)
    source_halo = halo_copies(1, S0, X0, H0, Y0, 2, 2, 2)
    beta1_halo = halo_copies(2, B1, X0 // 2, H1, Y0 // 2, 5, 5, 5)
    beta_late = late_copies(0, B0, LX0.at[0], LY0.at[0], X0, H0, Y0, 3, 4)
    source_late = late_copies(1, S0, LX0.at[1], LY0.at[1], X0, H0, Y0, 2, 3)
    start_all(beta_halo)
    start_all(source_halo)
    tell(0)
    start_all(beta1_halo)
    beta2_window = window_copies(0, PB, GB)
    start_all(beta2_window)

    def setup(level, Bl, CX, CY, CM, CP, Q, D, first, last, row, rows, hx, nx, ny):
        apart = 1 << level
        h = 0.5 * 0.25**level

        def plane(i, carry):
            at = pl.ds(row, rows)
            c = Bl[i, at]
            xm = Bl[i - 1, at]
            xp = Bl[i + 1, at]
            ym = Bl[i, pl.ds(row - 1, rows)]
            yp = Bl[i, pl.ds(row + 1, rows)]
            lane = lane_of(c.shape)
            low = lane >= apart
            high = lane < LANES - apart
            zm = jnp.where(low, roll(c, apart, 1), 0.0)
            zp = jnp.where(high, roll(c, -apart, 1), 0.0)
            CX[i, at] = h * (c + xm)
            CY[i, at] = h * (c + ym)
            CM[i, at] = jnp.where(low, h * (c + zm), 0.0)
            CP[i, at] = jnp.where(high, h * (c + zp), 0.0)
            d = h * (6.0 * c + ((xm + xp) + (ym + yp) + (zm + zp)))
            D[i, at] = d
            x = g * nx + i - hx
            y = lax.broadcasted_iota(jnp.int32, c.shape, 0) + (b * ny + row - HY)
            inside = (y >= 0) & (y < B * ny) & (x >= 0) & (x < G * nx)
            Q[i, at] = jnp.where(inside, W / d, 0.0)
            return carry

        lax.fori_loop(first, last, plane, 0, unroll=True)

    def across(level, V, CX, CY, CM, CP, i, row, rows):
        apart = 1 << level
        at = pl.ds(row, rows)
        up = pl.ds(row + 1, rows)
        v = V[i, at]
        total = CX[i, at] * V[i - 1, at] + CX[i + 1, at] * V[i + 1, at]
        total = total + (CY[i, at] * V[i, pl.ds(row - 1, rows)] + CY[i, up] * V[i, up])
        total = total + (CM[i, at] * roll(v, apart, 1) + CP[i, at] * roll(v, -apart, 1))
        return v, total

    def first_sweep(V, Q, S, first, last, row, rows):
        def plane(i, carry):
            V[i, pl.ds(row, rows)] = Q[i, pl.ds(row, rows)] * S[i, pl.ds(row, rows)]
            return carry

        lax.fori_loop(first, last, plane, 0, unroll=True)

    def sweep(level, V, U, S, Q, coeffs, first, last, row, rows, drop_x=0, drop_y=0):
        def plane(i, carry):
            v, total = across(level, V, *coeffs, i, row, rows)
            U[i - drop_x, pl.ds(row - drop_y, rows)] = (1.0 - W) * v + Q[i, pl.ds(row, rows)] * (
                S[i, pl.ds(row, rows)] + total
            )
            return carry

        lax.fori_loop(first, last, plane, 0, unroll=True)

    def residual(level, V, S, D, coeffs, i, row, rows):
        v, total = across(level, V, *coeffs, i, row, rows)
        return S[i, pl.ds(row, rows)] - (D[i, pl.ds(row, rows)] * v - total)

    coeffs0 = (CX0, CY0, CM0, CP0)
    coeffs1 = (CX1, CY1, CM1, CP1)
    row0, rows0 = 4, 40
    row1, rows1 = 4, 24

    recv_all(beta_halo)
    hear(0)
    tell(1)
    setup(0, B0, CX0, CY0, CM0, CP0, Q0, D0, 2, 22, row0, rows0, H0, X0, Y0)
    recv_all(source_halo)
    first_sweep(V0, Q0, S0, 2, 22, row0, rows0)
    sweep(0, V0, U0, S0, Q0, coeffs0, 3, 21, row0, rows0)

    def down0(p, carry):
        i = H0 + 2 * p
        pair = residual(0, U0, S0, D0, coeffs0, i, HY, Y0) + residual(0, U0, S0, D0, coeffs0, i + 1, HY, Y0)
        half = halve(pair, 1, p)
        S1[H1 + p, pl.ds(HY, Y0 // 2)] = half
        SZ1[H1 + p, pl.ds(HY, Y0 // 2)] = half
        return carry

    lax.fori_loop(0, X0 // 2, down0, 0, unroll=True)
    source1_halo = halo_copies(3, S1, X0 // 2, H1, Y0 // 2, 2, 2, 4)
    source1_late = late_copies(2, S1, LX1, LY1, X0 // 2, H1, Y0 // 2, 2, 4)
    start_all(source1_halo)
    def neighbours(v, level):
        st, zs = 1 << (level - 2), 1 << level
        before = [v[i - 1] for i in range(G)]
        after = [v[(i + 1) % G] for i in range(G)]
        if st == 4:
            xm, xp = before, after
        else:
            k = lane_of(v[0].shape) & 3
            xm = [jnp.where(k >= st, roll(v[i], st, 1), roll(before[i], st - 4, 1)) for i in range(G)]
            xp = [jnp.where(k < 4 - st, roll(v[i], -st, 1), roll(after[i], 4 - st, 1)) for i in range(G)]
        ym = [roll(a, 1, 0) for a in v]
        yp = [roll(a, -1, 0) for a in v]
        zm = [roll(a, zs, 1) for a in v]
        zp = [roll(a, -zs, 1) for a in v]
        return xm, xp, ym, yp, zm, zp

    def setup_whole(beta, C, level, first, total_rows):
        st, zs = 1 << (level - 2), 1 << level
        h = 0.5 * 0.25**level
        near = neighbours(beta, level)
        shape = beta[0].shape
        lane = lane_of(shape)
        row = lax.broadcasted_iota(jnp.int32, shape, 0) + first
        inside = (row >= 0) & (row < total_rows)
        for i in range(G):
            ok = [
                inside & ((lane & 3) >= st) if i == 0 else inside,
                inside & ((lane & 3) < 4 - st) if i == G - 1 else inside,
                (row > 0) & (row < total_rows),
                (row >= 0) & (row < total_rows - 1),
                inside & (lane >= zs),
                inside & (lane < LANES - zs),
            ]
            total = 6.0 * beta[i]
            for d in range(6):
                there = jnp.where(ok[d], near[d][i], 0.0)
                total = total + there
                C[d, i] = jnp.where(ok[d], h * (beta[i] + there), 0.0)
            diag = h * total
            C[6, i] = diag
            C[7, i] = jnp.where(inside, W / diag, 0.0)

    def sum_across(v, C, level):
        near = neighbours(v, level)
        out = []
        for i in range(G):
            out.append(
                (C[0, i] * near[0][i] + C[1, i] * near[1][i])
                + (C[2, i] * near[2][i] + C[3, i] * near[3][i])
                + (C[4, i] * near[4][i] + C[5, i] * near[5][i])
            )
        return out

    def sweep_whole(v, s, C, level):
        total = sum_across(v, C, level)
        return [(1.0 - W) * v[i] + C[7, i] * (s[i] + total[i]) for i in range(G)]

    def coarsen(v, level):
        st, zs = 1 << (level - 2), 1 << level
        rows = v[0].shape[0]
        out = []
        for i in range(G):
            E[i, pl.ds(0, rows)] = pair_lanes(pair_lanes(v[i], st), zs)
            out.append(0.125 * (E[i, pl.ds(0, rows // 2, stride=2)] + E[i, pl.ds(1, rows // 2, stride=2)]))
        return out

    def refine(v):
        rows = v[0].shape[0]
        out = []
        for i in range(G):
            E[i, pl.ds(0, rows, stride=2)] = v[i]
            E[i, pl.ds(1, rows, stride=2)] = v[i]
            out.append(E[i, pl.ds(0, 2 * rows)])
        return out

    recv_all(beta1_halo)
    setup(1, B1, CX1, CY1, CM1, CP1, Q1, D1, 1, 17, row1, rows1, H1, X0 // 2, Y0 // 2)
    first_sweep(V1, Q1, SZ1, H1, H1 + X0 // 2, HY, Y0 // 2)
    sweep(1, V1, U1, SZ1, Q1, coeffs1, H1 - 1, H1 + X0 // 2 + 1, HY - 2, Y0 // 2 + 4)
    planes = []
    for p in range(-1, X0 // 4 + 1):
        i = H1 + 2 * p
        pair = residual(1, U1, SZ1, D1, coeffs1, i, HY - 2, Y0 // 2 + 4)
        pair = pair + residual(1, U1, SZ1, D1, coeffs1, i + 1, HY - 2, Y0 // 2 + 4)
        planes.append(halve(pair, 2, p + 1))
    k = lane_of(planes[0].shape) & 3
    Z2[g, pl.ds(7, 10)] = jnp.where(k == 3, planes[0], 0.0)
    Z2[g + 1, pl.ds(7, 10)] = pack(planes[1:5])
    Z2[g + 2, pl.ds(7, 10)] = jnp.where(k == 0, planes[5], 0.0)
    recv_all(beta2_window)
    setup_whole([GB[i] for i in range(G)], C2, 2, 8 * b - 8, ry2)
    z2 = [Z2[i + 1] for i in range(G)]
    v = [C2[7, i] * z2[i] for i in range(G)]
    v = sweep_whole(v, z2, C2, 2)
    total = sum_across(v, C2, 2)
    for i in range(G):
        E[i, pl.ds(0, 24)] = pair_lanes(pair_lanes(z2[i] - (C2[6, i] * v[i] - total[i]), 1), 4)
        F[i + 1] = 0.125 * (E[i, pl.ds(4, 8, stride=2)] + E[i, pl.ds(5, 8, stride=2)])
    slot = (lane_of((8, LANES)) & 1) + ((lane_of((8, LANES)) >> 1) & 2)
    packed = jnp.where(slot == 2, F[g + 2], P3[...])
    packed = jnp.where(slot == 1, F[g + 1], packed)
    PG[...] = jnp.where(slot == 0, F[g], packed)
    hear(1)
    gather_start()
    start_all(source1_late[0])
    start_all(beta_late[0])
    start_all(source_late[0])

    recv_all(source1_halo)
    first_sweep(V1, Q1, S1, 3, 15, row1, rows1)
    sweep(1, V1, U1, S1, Q1, coeffs1, 4, 14, row1, rows1)
    planes = []
    for p in range(X0 // 4):
        i = H1 + 2 * p
        pair = residual(1, U1, S1, D1, coeffs1, i, HY, Y0 // 2) + residual(1, U1, S1, D1, coeffs1, i + 1, HY, Y0 // 2)
        planes.append(halve(pair, 2, p))
    PS[...] = pack(planes)
    source2_window = window_copies(1, PS, GS)
    start_all(source2_window)
    GS[g, pl.ds(8, 8)] = PS[...]

    land_all(source1_late)
    first_sweep(V1, Q1, S1, 1, 17, row1, rows1)
    sweep(1, V1, U1, S1, Q1, coeffs1, 2, 16, row1, rows1)
    land_all(beta_late)
    land_all(source_late)
    setup(0, B0, CX0, CY0, CM0, CP0, Q0, D0, 1, 23, row0, rows0, H0, X0, Y0)
    first_sweep(V0, Q0, S0, 1, 23, row0, rows0)
    sweep(0, V0, U0, S0, Q0, coeffs0, 2, 22, row0, rows0)

    gather_recv()
    slot = (lane_of((ry3, LANES)) & 1) + ((lane_of((ry3, LANES)) >> 1) & 2)
    parts = [GE[0, i, pl.ds(10, ry3)] + GE[1, i, pl.ds(6, ry3)] for i in range(G)]

    def spread(v):
        return pair_lanes(pair_lanes(v, 1), 4)

    beta3 = [spread(jnp.where(slot == 3, a, 0.0)) for a in parts]
    s3 = []
    for i in range(G):
        mine = jnp.where(slot == 1, parts[i], 0.0)
        if i + 1 < G:
            mine = jnp.where(slot == 0, parts[i + 1], mine)
        if i > 0:
            mine = jnp.where(slot == 2, parts[i - 1], mine)
        s3.append(spread(mine))
    setup_whole(beta3, C3, 3, 0, ry3)
    beta4 = coarsen(beta3, 3)
    setup_whole(beta4, C4, 4, 0, ry4)

    v = [C3[7, i] * s3[i] for i in range(G)]
    v = sweep_whole(v, s3, C3, 3)
    for i in range(G):
        F3[0, i] = v[i]
        F3[1, i] = s3[i]
    total = sum_across(v, C3, 3)
    s4 = coarsen([s3[i] - (C3[6, i] * v[i] - total[i]) for i in range(G)], 3)

    def dot(a, c):
        acc = a[0] * c[0]
        for i in range(1, G):
            acc = acc + a[i] * c[i]
        part = acc[0:8]
        for j in range(8, ry4, 8):
            part = part + acc[j : j + 8]
        return jnp.sum(jnp.sum(part, axis=0, keepdims=True), axis=1, keepdims=True)

    def cg(step, carry):
        x, r, p, rr = carry
        near = sum_across(p, C4, 4)
        q = [C4[6, i] * p[i] - near[i] for i in range(G)]
        alpha = rr / dot(p, q)
        x = [x[i] + alpha * p[i] for i in range(G)]
        r = [r[i] - alpha * q[i] for i in range(G)]
        new = dot(r, r)
        ratio = new / rr
        p = [r[i] + ratio * p[i] for i in range(G)]
        return x, r, p, new

    zero = [jnp.zeros((ry4, LANES), F32) for i in range(G)]
    x4 = lax.fori_loop(0, COARSE, cg, (zero, s4, s4, dot(s4, s4)), unroll=True)[0]

    up = refine(x4)
    s3 = [F3[1, i] for i in range(G)]
    v = [F3[0, i] + up[i] for i in range(G)]
    for _ in range(SWEEPS):
        v = sweep_whole(v, s3, C3, 3)
    for i in range(G):
        for odd in (0, 1):
            E2[i, pl.ds(8 + odd, ry3, stride=2)] = v[i]
    recv_all(source2_window)
    s2 = [GS[i] for i in range(G)]
    v = [C2[7, i] * s2[i] for i in range(G)]
    v = sweep_whole(v, s2, C2, 2)
    v = [v[i] + E2[i, pl.ds(pl.multiple_of(b * 8, 8), 24)] for i in range(G)]
    for _ in range(SWEEPS):
        v = sweep_whole(v, s2, C2, 2)
    for i in range(G):
        V2[i + 1] = v[i]

    for x2 in range(-2, 6):
        k = x2 % 4
        window = V2[g + 1 + x2 // 4]
        one = jnp.where((lane_of(window.shape) & 3) == k, window, 0.0)
        one = one + roll(one, 1 if k in (0, 2) else -1, 1)
        one = one + roll(one, 2 if k in (0, 1) else -2, 1)
        T[x2 + 2, pl.ds(0, 24)] = one
    for x2 in range(-2, 6):
        add = T[x2 + 2, pl.ds(6, 12)]
        for i in (2 * x2 + 5, 2 * x2 + 6):
            if 2 <= i < 16:
                for odd in (0, 1):
                    at = pl.ds(row1 + odd, 12, stride=2)
                    U1[i, at] = U1[i, at] + add
    sweep(1, U1, V1, S1, Q1, coeffs1, 3, 15, row1, rows1)
    sweep(1, V1, U1, S1, Q1, coeffs1, 4, 14, row1, rows1)

    def prolong0(i, carry):
        add = U1[i + 3, pl.ds(6, 20)]
        for half in (0, 1):
            for odd in (0, 1):
                at = pl.ds(row0 + odd, 20, stride=2)
                U0[2 * i + half, at] = U0[2 * i + half, at] + add
        return carry

    lax.fori_loop(1, 11, prolong0, 0, unroll=True)
    sweep(0, U0, V0, S0, Q0, coeffs0, 3, 21, row0, rows0)
    sweep(0, V0, out_ref, S0, Q0, coeffs0, 4, 20, HY, Y0, H0, HY)

    sent_all(beta_halo)
    sent_all(source_halo)
    sent_all(beta1_halo)
    sent_all(source1_halo)
    sent_all(beta_late[0])
    sent_all(source_late[0])
    sent_all(source1_late[0])
    sent_all(beta2_window)
    sent_all(source2_window)
    gather_sent()


def in_one_kernel(G, B, right_side, beta):
    level0 = pltpu.VMEM((X0 + 2 * H0, Y0 + 2 * HY, LANES), F32)
    level1 = pltpu.VMEM((X0 // 2 + 2 * H1, Y0 // 2 + 2 * HY, LANES), F32)
    return pl.pallas_call(
        functools.partial(kernel, G, B),
        out_shape=jax.ShapeDtypeStruct(right_side.shape, F32),
        in_specs=[pl.BlockSpec(memory_space=pltpu.HBM)] * 2,
        out_specs=pl.BlockSpec(memory_space=pltpu.VMEM),
        scratch_shapes=[level0] * 10
        + [level1] * 10
        + [
            pltpu.VMEM((8, Y0, LANES), F32),
            level1,
            pltpu.VMEM((8, LANES), F32),
            pltpu.VMEM((8, LANES), F32),
            pltpu.VMEM((8, LANES), F32),
            pltpu.VMEM((8, LANES), F32),
            pltpu.VMEM((G, 24, LANES), F32),
            pltpu.VMEM((G, 24, LANES), F32),
            pltpu.VMEM((2, G, 4 * B + 16, LANES), F32),
            pltpu.VMEM((G + 2, 24, LANES), F32),
            pltpu.VMEM((G + 2, 24, LANES), F32),
            pltpu.VMEM((8, G, 24, LANES), F32),
            pltpu.VMEM((8, G, 4 * B, LANES), F32),
            pltpu.VMEM((8, G, 2 * B, LANES), F32),
            pltpu.VMEM((G, 8 * B, LANES), F32),
            pltpu.VMEM((G, 8 * B + 16, LANES), F32),
            pltpu.VMEM((G + 2, 8, LANES), F32),
            pltpu.VMEM((2, G, 4 * B, LANES), F32),
            pltpu.VMEM((2, 2, 1, Y0, LANES), F32),
            pltpu.VMEM((2, 2, X0, 8, LANES), F32),
            pltpu.VMEM((2, 2, Y0 // 2, LANES), F32),
            pltpu.VMEM((2, X0 // 2, 8, LANES), F32),
            pltpu.SemaphoreType.DMA((4, 8)),
            pltpu.SemaphoreType.DMA((4, 8)),
            pltpu.SemaphoreType.DMA((3, 4)),
            pltpu.SemaphoreType.DMA((3, 4)),
            pltpu.SemaphoreType.DMA((2, 3 * G)),
            pltpu.SemaphoreType.DMA((2, 3 * G)),
            pltpu.SemaphoreType.DMA((G * B,)),
            pltpu.SemaphoreType.DMA((1,)),
            pltpu.SemaphoreType.REGULAR((2,)),
            pltpu.SemaphoreType.DMA((2,)),
        ],
        compiler_params=pltpu.CompilerParams(
            collective_id=0, has_side_effects=True, vmem_limit_bytes=40 * 1024 * 1024
        ),
    )(*(pltpu.with_memory_space_constraint(a, pltpu.HBM) for a in (right_side, beta)))


relax_weight = 2.0 / 3.0


def with_halo(shard, sides, width):
    for axis, dim in sides:
        size, length = (lax.axis_size(axis), shard.shape[dim])
        up = [(i, (i + 1) % size) for i in range(size - 1)]
        down = [(j, i) for i, j in up]
        last = lax.slice_in_dim(shard, length - width, length, axis=dim)
        leading = lax.slice_in_dim(shard, 0, width, axis=dim)
        before = lax.ppermute(last, axis, up)
        after = lax.ppermute(leading, axis, down)
        shard = jnp.concatenate([before, shard, after], axis=dim)
    return shard


def from_partner(block, axis, apart):
    count = lax.axis_size(axis)
    route = []
    for low in range(count):
        high = low | 1 << apart
        if high != low and high < count:
            route += [(low, high), (high, low)]
    return lax.ppermute(block, axis, route)


def pad_zeros(field):
    return jnp.pad(field, 1)


def pad_local(field):
    extended = with_halo(field, (("grp", 0), ("box", 1)), 1)
    return jnp.pad(extended, ((0, 0), (0, 0), (1, 1)))


def face_coeffs(padded_beta):
    face_x = 0.5 * (padded_beta[1:, 1:-1, 1:-1] + padded_beta[:-1, 1:-1, 1:-1])
    face_y = 0.5 * (padded_beta[1:-1, 1:, 1:-1] + padded_beta[1:-1, :-1, 1:-1])
    face_z = 0.5 * (padded_beta[1:-1, 1:-1, 1:] + padded_beta[1:-1, 1:-1, :-1])
    return (face_x, face_y, face_z)


def inverse_diagonal(coeffs, scale):
    face_x, face_y, face_z = coeffs
    total = (
        face_x[:-1]
        + face_x[1:]
        + face_y[:, :-1]
        + face_y[:, 1:]
        + face_z[:, :, :-1]
        + face_z[:, :, 1:]
    )
    return 1.0 / (scale * total)


def apply_operator(padded, coeffs, scale):
    face_x, face_y, face_z = coeffs
    centre = padded[1:-1, 1:-1, 1:-1]
    total = face_x[:-1] * (centre - padded[:-2, 1:-1, 1:-1]) + face_x[1:] * (
        centre - padded[2:, 1:-1, 1:-1]
    )
    total = (
        total
        + face_y[:, :-1] * (centre - padded[1:-1, :-2, 1:-1])
        + face_y[:, 1:] * (centre - padded[1:-1, 2:, 1:-1])
    )
    total = (
        total
        + face_z[:, :, :-1] * (centre - padded[1:-1, 1:-1, :-2])
        + face_z[:, :, 1:] * (centre - padded[1:-1, 1:-1, 2:])
    )
    return scale * total


def jacobi_sweeps(field, source, coeffs, inverse, scale, count, padder):
    for sweep_index in range(count):
        field = (
            field + relax_weight * (source - apply_operator(padder(field), coeffs, scale)) * inverse
        )
    return field


def conjugate_solve(source, coeffs, scale, count):
    field = jnp.zeros_like(source)
    remain = source
    direction = source
    norm_now = jnp.sum(remain * remain)
    for step_index in range(count):
        image = apply_operator(pad_zeros(direction), coeffs, scale)
        alpha = norm_now / jnp.sum(direction * image)
        field = field + alpha * direction
        remain = remain - alpha * image
        norm_next = jnp.sum(remain * remain)
        direction = remain + norm_next / norm_now * direction
        norm_now = norm_next
    return field


def restrict_mean(field):
    size_a, size_b, size_c = field.shape
    blocks = field.reshape(size_a // 2, 2, size_b // 2, 2, size_c // 2, 2)
    return jnp.mean(blocks, axis=(1, 3, 5))


def prolong_copy(field):
    return jnp.repeat(jnp.repeat(jnp.repeat(field, 2, axis=0), 2, axis=1), 2, axis=2)


def merge_groups(pieces):
    group_index = lax.axis_index("grp")
    for bit_index in range(lax.axis_size("grp").bit_length() - 1):
        partner = from_partner(pieces, "grp", bit_index)
        upper = group_index >> bit_index & 1 == 1
        pieces = tuple(
            (
                jnp.where(
                    upper,
                    jnp.concatenate([theirs, own_piece], 0),
                    jnp.concatenate([own_piece, theirs], 0),
                )
                for own_piece, theirs in zip(pieces, partner)
            )
        )
    return pieces


def merge_boxes(pieces):
    return lax.all_gather(pieces, "box", axis=1, tiled=True)


def shards(right_side, beta):
    source = right_side
    level_beta = beta
    saved = []
    for level in range(LEVELS):
        scale = 0.25**level
        coeffs = face_coeffs(pad_local(level_beta))
        inverse = inverse_diagonal(coeffs, scale)
        field = relax_weight * source * inverse
        field = jacobi_sweeps(field, source, coeffs, inverse, scale, SWEEPS - 1, pad_local)
        residual = source - apply_operator(pad_local(field), coeffs, scale)
        saved.append((field, source, coeffs, inverse, scale))
        source = restrict_mean(residual)
        level_beta = restrict_mean(level_beta)
    low_scale = 0.25**LEVELS
    whole_source, whole_beta = merge_boxes(merge_groups((source, level_beta)))
    low_coeffs = face_coeffs(pad_zeros(whole_beta))
    whole_field = conjugate_solve(whole_source, low_coeffs, low_scale, COARSE)
    block_a, block_b, block_c = source.shape
    field = lax.dynamic_slice(
        whole_field,
        (lax.axis_index("grp") * block_a, lax.axis_index("box") * block_b, 0),
        (block_a, block_b, block_c),
    )
    for level in range(LEVELS - 1, -1, -1):
        kept, level_source, coeffs, inverse, scale = saved[level]
        field = kept + prolong_copy(field)
        field = jacobi_sweeps(field, level_source, coeffs, inverse, scale, SWEEPS, pad_local)
    return field


def solution(mesh):
    placed = P("grp", "box", None)
    G, B = mesh.shape["grp"], mesh.shape["box"]
    small = (G, B) in ((4, 8), (8, 8), (4, 16), (8, 4), (2, 16))

    def local(right_side, beta):
        if small and right_side.shape == (X0, Y0, LANES):
            return in_one_kernel(G, B, right_side, beta)
        return shards(right_side, beta)

    return jax.shard_map(local, mesh=mesh, in_specs=(placed, placed), out_specs=placed, check_vma=False)
```

```python
import functools

import jax
import jax.numpy as jnp
from jax import lax
from jax.experimental import pallas as pl
from jax.experimental.pallas import tpu as pltpu
from jax.sharding import PartitionSpec as P

LEVELS = 4
SWEEPS = 2
COARSE = 8
W = 2.0 / 3.0
MESH = pl.DeviceIdType.MESH
F32 = jnp.float32

X0, Y0, LANES = 16, 32, 128
H0 = 4
H1 = 5
HY = 8
DIRS = [(dx, dy) for dx in (-1, 0, 1) for dy in (-1, 0, 1) if (dx, dy) != (0, 0)]


def roll(v, shift, axis):
    return pltpu.roll(v, shift % v.shape[axis], axis)


def lane_of(shape):
    return lax.broadcasted_iota(jnp.int32, shape, len(shape) - 1)


def pair_lanes(v, apart):
    lane = lane_of(v.shape)
    return v + jnp.where((lane & apart) == 0, roll(v, -apart, 1), roll(v, apart, 1))


def span(size, halo, step, near, far):
    if step == 0:
        return (halo, size), (halo, size)
    if step < 0:
        return (halo + near, far - near), (halo + size + near, far - near)
    return (halo + size - far, far - near), (halo - far, far - near)


def kernel(
    G, B, rs_ref, be_ref, out_ref,
    B0, S0, V0, U0, CX0, CY0, CM0, CP0, Q0, D0,
    B1, S1, V1, U1, CX1, CY1, CM1, CP1, Q1, D1,
    T, SZ0, SZ1, PB, PS, P3, PG, GB, GS, GL, GE, V2, Z2, C2, C3, C4, E, E2, F, F3, LX0, LY0, LX1, LY1,
    halo_send, halo_recv, late_send, late_recv, win_send, win_recv, ga_send, ga_recv, rounds, loc_sem,
):
    n = G * B
    g = lax.axis_index("grp")
    b = lax.axis_index("box")
    me = g * B + b
    ry2, ry3, ry4 = 8 * B, 4 * B, 2 * B

    own0 = (pl.ds(H0, X0), pl.ds(HY, Y0))
    load_b = pltpu.make_async_copy(be_ref, B0.at[own0[0], own0[1]], loc_sem.at[0])
    load_s = pltpu.make_async_copy(rs_ref, S0.at[own0[0], own0[1]], loc_sem.at[1])
    load_b.start()
    load_s.start()
    load_z = pltpu.make_async_copy(rs_ref, SZ0.at[own0[0], own0[1]], loc_sem.at[2])
    load_z.start()

    barrier = pltpu.get_barrier_semaphore()

    expected = 0
    for dx, dy in DIRS:
        there = (g + dx >= 0) & (g + dx < G) & (b + dy >= 0) & (b + dy < B)
        expected = expected + there.astype(jnp.int32)

        @pl.when(there)
        def _():
            pl.semaphore_signal(barrier, inc=1, device_id=(g + dx, b + dy), device_id_type=MESH)

    reach = max(1, -(-(B - 2) // 3))
    others = []
    for far in range(2, G):
        for dx in (-far, far):
            others += [(dx, dy) for dy in (-1, 0, 1)]
    for far in range(2, reach + 1):
        others += [(0, -far), (0, far)]
    for dx, dy in others:
        there = (g + dx >= 0) & (g + dx < G) & (b + dy >= 0) & (b + dy < B)
        expected = expected + there.astype(jnp.int32)

        @pl.when(there)
        def _():
            pl.semaphore_signal(barrier, inc=1, device_id=(g + dx, b + dy), device_id_type=MESH)

    def boxes_of(k):
        for far in range(k * reach + 1, (k + 1) * reach + 1):
            for dy in (-far, far):
                yield b + dy, (b + dy >= 0) & (b + dy < B)

    def tell(k):
        for other, there in boxes_of(k):

            @pl.when(there)
            def _():
                pl.semaphore_signal(rounds.at[k], inc=1, device_id=(g, other), device_id_type=MESH)

    def hear(k):
        count = 0
        for _, there in boxes_of(k):
            count = count + there.astype(jnp.int32)
        pl.semaphore_wait(rounds.at[k], count)

    for ref, nx, hx, ny in ((B0, X0, H0, Y0), (S0, X0, H0, Y0), (B1, X0 // 2, H1, Y0 // 2), (S1, X0 // 2, H1, Y0 // 2)):
        rows = ny + 2 * HY
        planes = nx + 2 * hx

        @pl.when(g == 0)
        def _():
            ref[pl.ds(0, hx)] = jnp.zeros((hx, rows, LANES), F32)

        @pl.when(g == G - 1)
        def _():
            ref[pl.ds(hx + nx, hx)] = jnp.zeros((hx, rows, LANES), F32)

        @pl.when(b == 0)
        def _():
            ref[:, pl.ds(0, HY)] = jnp.zeros((planes, HY, LANES), F32)

        @pl.when(b == B - 1)
        def _():
            ref[:, pl.ds(HY + ny, HY)] = jnp.zeros((planes, HY, LANES), F32)

    load_b.wait()

    def halve(pair, apart, slot):
        rows = pair.shape[0]
        T[slot, pl.ds(0, rows)] = pair_lanes(pair, apart)
        return 0.125 * (T[slot, pl.ds(0, rows // 2, stride=2)] + T[slot, pl.ds(1, rows // 2, stride=2)])

    def pack(planes):
        lane = lane_of(planes[0].shape) & 3
        packed = planes[3]
        for k in (2, 1, 0):
            packed = jnp.where(lane == k, planes[k], packed)
        return packed

    for p in range(X0 // 2):
        B1[H1 + p, pl.ds(HY, Y0 // 2)] = halve(
            B0[H0 + 2 * p, pl.ds(HY, Y0)] + B0[H0 + 2 * p + 1, pl.ds(HY, Y0)], 1, p
        )
    PB[...] = pack([
        halve(B1[H1 + 2 * p, pl.ds(HY, Y0 // 2)] + B1[H1 + 2 * p + 1, pl.ds(HY, Y0 // 2)], 2, p)
        for p in range(X0 // 4)
    ])
    GB[g, pl.ds(8, 8)] = PB[...]
    T[0, pl.ds(0, 8)] = pair_lanes(pair_lanes(PB[...], 1), 4)
    P3[...] = jnp.zeros((8, LANES), F32)
    P3[pl.ds(2, 4)] = 0.125 * (T[0, pl.ds(0, 4, stride=2)] + T[0, pl.ds(1, 4, stride=2)])

    load_s.wait()
    load_z.wait()
    pl.semaphore_wait(barrier, expected)

    def there_from(dx, dy):
        return (g + dx >= 0) & (g + dx < G) & (b + dy >= 0) & (b + dy < B)

    def halo_copies(kind, ref, nx, hx, ny, deep, tall, corner):
        made = []
        for at, (dx, dy) in enumerate(DIRS):
            (sx, lx), (tx, _) = span(nx, hx, dx, 0, deep if dy == 0 else corner)
            (sy, ly), (ty, _) = span(ny, HY, dy, 0, tall if dx == 0 else corner)
            copy = pltpu.make_async_remote_copy(
                src_ref=ref.at[pl.ds(sx, lx), pl.ds(sy, ly)],
                dst_ref=ref.at[pl.ds(tx, lx), pl.ds(ty, ly)],
                send_sem=halo_send.at[kind, at],
                recv_sem=halo_recv.at[kind, at],
                device_id=(g + dx, b + dy),
                device_id_type=MESH,
            )
            made.append((copy, there_from(dx, dy), there_from(-dx, -dy)))
        return made

    def late_copies(kind, ref, LX, LY, nx, hx, ny, near, far):
        made, land = [], []
        for at, (dx, dy) in enumerate(((-1, 0), (1, 0), (0, -1), (0, 1))):
            (sx, lx), (tx, _) = span(nx, hx, dx, near, far)
            (sy, ly), (ty, _) = span(ny, HY, dy, near, far)
            box = LX.at[at] if dy == 0 else LY.at[at - 2, :, pl.ds(0, far - near)]
            copy = pltpu.make_async_remote_copy(
                src_ref=ref.at[pl.ds(sx, lx), pl.ds(sy, ly)],
                dst_ref=box,
                send_sem=late_send.at[kind, at],
                recv_sem=late_recv.at[kind, at],
                device_id=(g + dx, b + dy),
                device_id_type=MESH,
            )
            here = there_from(-dx, -dy)
            made.append((copy, there_from(dx, dy), here))

            def put(tx=tx, lx=lx, ty=ty, ly=ly, box=box):
                ref[pl.ds(tx, lx), pl.ds(ty, ly)] = box[...]

            land.append((here, put))
        return made, land

    def land_all(late):
        made, land = late
        for (copy, _, here), (_, put) in zip(made, land):

            @pl.when(here)
            def _():
                copy.wait_recv()
                put()

    def start_all(copies):
        for copy, there, _ in copies:
            pl.when(there)(copy.start)

    def recv_all(copies):
        for copy, _, here in copies:
            pl.when(here)(copy.wait_recv)

    def sent_all(copies):
        for copy, there, _ in copies:
            pl.when(there)(copy.wait_send)

    def window_copies(kind, packed, spot):
        made = []
        for o in range(G):
            for dy in (-1, 0, 1):
                if (o, dy) == (0, 0):
                    continue
                at = 3 * o + dy + 1
                copy = pltpu.make_async_remote_copy(
                    src_ref=packed(dy),
                    dst_ref=spot(dy),
                    send_sem=win_send.at[kind, at],
                    recv_sem=win_recv.at[kind, at],
                    device_id=((g + o) % G, b + dy),
                    device_id_type=MESH,
                )
                made.append((copy, (b + dy >= 0) & (b + dy < B), (b - dy >= 0) & (b - dy < B)))
        return made

    def gather_start():
        spot = GE.at[b % 2, g, pl.ds(pl.multiple_of(8 + 8 * (b // 2), 8), 8)]
        pltpu.make_async_copy(PG, spot, ga_recv.at[0]).start()

        def one(d, carry):
            peer = (me + d) % n
            pltpu.make_async_remote_copy(
                src_ref=PG,
                dst_ref=spot,
                send_sem=ga_send.at[0],
                recv_sem=ga_recv.at[0],
                device_id=(peer // B, peer % B),
                device_id_type=MESH,
            ).start()
            return carry

        lax.fori_loop(1, n, one, 0, unroll=True)

    def gather_recv():
        whole = GE.at[:, :, pl.ds(8, ry3)]
        pltpu.make_async_copy(whole, whole, ga_recv.at[0]).wait()

    def gather_sent():
        room = CX0.at[pl.ds(0, 8), pl.ds(0, n - 1)]
        pltpu.make_async_copy(room, room, ga_send.at[0]).wait()

    beta_halo = halo_copies(0, B0, X0, H0, Y0, 2, 2, 3)
    source_halo = halo_copies(1, S0, X0, H0, Y0, 3, 3, 2)
    beta1_halo = halo_copies(2, B1, X0 // 2, H1, Y0 // 2, 3, 3, 5)
    beta2_window = window_copies(0, lambda dy: PB, lambda dy: GB.at[g, pl.ds(8 - 8 * dy, 8)])
    beta_late = late_copies(0, B0, LX0, LY0, X0, H0, Y0, 2, 4)
    beta1_late = late_copies(1, B1, LX1, LY1, X0 // 2, H1, Y0 // 2, 3, 5)
    start_all(beta_halo)

    for ref in (SZ1, V1, U1, V2, Z2, GS):
        ref[...] = jnp.zeros(ref.shape, F32)
    for ref, deep in ((SZ0, 2), (V0, 2), (U0, 3)):
        for x in (H0 - deep, H0 + X0 + deep - 2):
            ref[pl.ds(x, 2)] = jnp.zeros((2, Y0 + 2 * HY, LANES), F32)
        for y in (0, HY + Y0):
            ref[pl.ds(H0 - 1, X0 + 2), pl.ds(y, HY)] = jnp.zeros((X0 + 2, HY, LANES), F32)
    for ref, nx, hx, ny, near in ((B0, X0, H0, Y0, 2), (B1, X0 // 2, H1, Y0 // 2, 3)):
        for x in (hx - near - 2, hx + nx + near):
            ref[pl.ds(x, 2), pl.ds(HY, ny)] = jnp.zeros((2, ny, LANES), F32)
        for y in (HY - near - 2, HY + ny + near):
            ref[pl.ds(hx, nx), pl.ds(y, 2)] = jnp.zeros((nx, 2, LANES), F32)
    CY1[:, pl.ds(HY + Y0 // 2 + 4, 4)] = jnp.zeros((X0 // 2 + 2 * H1, 4, LANES), F32)
    for side, edge in ((0, 0), (2, B - 1)):

        @pl.when(b == edge)
        def _():
            GB[:, pl.ds(8 * side, 8)] = jnp.zeros((G, 8, LANES), F32)
            GL[:, side] = jnp.zeros((G, 2, 16, LANES), F32)

    E2[:, pl.ds(0, 8)] = jnp.zeros((G, 8, LANES), F32)
    E2[:, pl.ds(8 + ry2, 8)] = jnp.zeros((G, 8, LANES), F32)
    F[0] = jnp.zeros((8, LANES), F32)
    F[G + 1] = jnp.zeros((8, LANES), F32)
    GE[:, :, pl.ds(0, 8)] = jnp.zeros((2, G, 8, LANES), F32)
    GE[:, :, pl.ds(8 + ry3, 8)] = jnp.zeros((2, G, 8, LANES), F32)

    start_all(beta1_halo)
    start_all(beta2_window)
    tell(0)

    def setup(level, Bl, CX, CY, CM, CP, Q, D, first, last, row, rows, hx, nx, ny):
        apart = 1 << level
        h = 0.5 * 0.25**level

        def plane(i, carry):
            at = pl.ds(row, rows)
            c = Bl[i, at]
            xm = Bl[i - 1, at]
            xp = Bl[i + 1, at]
            ym = Bl[i, pl.ds(row - 1, rows)]
            yp = Bl[i, pl.ds(row + 1, rows)]
            lane = lane_of(c.shape)
            low = lane >= apart
            high = lane < LANES - apart
            zm = jnp.where(low, roll(c, apart, 1), 0.0)
            zp = jnp.where(high, roll(c, -apart, 1), 0.0)
            CX[i, at] = h * (c + xm)
            CY[i, at] = h * (c + ym)
            CM[i, at] = jnp.where(low, h * (c + zm), 0.0)
            CP[i, at] = jnp.where(high, h * (c + zp), 0.0)
            d = h * (6.0 * c + ((xm + xp) + (ym + yp) + (zm + zp)))
            D[i, at] = d
            x = g * nx + i - hx
            y = lax.broadcasted_iota(jnp.int32, c.shape, 0) + (b * ny + row - HY)
            inside = (y >= 0) & (y < B * ny) & (x >= 0) & (x < G * nx)
            Q[i, at] = jnp.where(inside, W / d, 0.0)
            return carry

        lax.fori_loop(first, last, plane, 0, unroll=True)

    def across(level, V, CX, CY, CM, CP, i, row, rows):
        apart = 1 << level
        at = pl.ds(row, rows)
        up = pl.ds(row + 1, rows)
        v = V[i, at]
        total = CX[i, at] * V[i - 1, at] + CX[i + 1, at] * V[i + 1, at]
        total = total + (CY[i, at] * V[i, pl.ds(row - 1, rows)] + CY[i, up] * V[i, up])
        total = total + (CM[i, at] * roll(v, apart, 1) + CP[i, at] * roll(v, -apart, 1))
        return v, total

    def first_sweep(V, Q, S, first, last, row, rows):
        def plane(i, carry):
            V[i, pl.ds(row, rows)] = Q[i, pl.ds(row, rows)] * S[i, pl.ds(row, rows)]
            return carry

        lax.fori_loop(first, last, plane, 0, unroll=True)

    def sweep(level, V, U, S, Q, coeffs, first, last, row, rows, drop_x=0, drop_y=0):
        def plane(i, carry):
            v, total = across(level, V, *coeffs, i, row, rows)
            U[i - drop_x, pl.ds(row - drop_y, rows)] = (1.0 - W) * v + Q[i, pl.ds(row, rows)] * (
                S[i, pl.ds(row, rows)] + total
            )
            return carry

        lax.fori_loop(first, last, plane, 0, unroll=True)

    def residual(level, V, S, D, coeffs, i, row, rows):
        v, total = across(level, V, *coeffs, i, row, rows)
        return S[i, pl.ds(row, rows)] - (D[i, pl.ds(row, rows)] * v - total)

    coeffs0 = (CX0, CY0, CM0, CP0)
    coeffs1 = (CX1, CY1, CM1, CP1)
    row0, rows0 = 4, 40
    row1, rows1 = 4, 24

    recv_all(beta_halo)
    hear(0)
    tell(1)
    start_all(source_halo)
    start_all(beta_late[0])
    start_all(beta1_late[0])
    def neighbours(v, level):
        st, zs = 1 << (level - 2), 1 << level
        before = [v[i - 1] for i in range(G)]
        after = [v[(i + 1) % G] for i in range(G)]
        if st == 4:
            xm, xp = before, after
        else:
            k = lane_of(v[0].shape) & 3
            xm = [jnp.where(k >= st, roll(v[i], st, 1), roll(before[i], st - 4, 1)) for i in range(G)]
            xp = [jnp.where(k < 4 - st, roll(v[i], -st, 1), roll(after[i], 4 - st, 1)) for i in range(G)]
        ym = [roll(a, 1, 0) for a in v]
        yp = [roll(a, -1, 0) for a in v]
        zm = [roll(a, zs, 1) for a in v]
        zp = [roll(a, -zs, 1) for a in v]
        return xm, xp, ym, yp, zm, zp

    def setup_whole(beta, C, level, first, total_rows):
        st, zs = 1 << (level - 2), 1 << level
        h = 0.5 * 0.25**level
        near = neighbours(beta, level)
        shape = beta[0].shape
        lane = lane_of(shape)
        row = lax.broadcasted_iota(jnp.int32, shape, 0) + first
        inside = (row >= 0) & (row < total_rows)
        for i in range(G):
            ok = [
                inside & ((lane & 3) >= st) if i == 0 else inside,
                inside & ((lane & 3) < 4 - st) if i == G - 1 else inside,
                (row > 0) & (row < total_rows),
                (row >= 0) & (row < total_rows - 1),
                inside & (lane >= zs),
                inside & (lane < LANES - zs),
            ]
            total = 6.0 * beta[i]
            for d in range(6):
                there = jnp.where(ok[d], near[d][i], 0.0)
                total = total + there
                C[d, i] = jnp.where(ok[d], h * (beta[i] + there), 0.0)
            diag = h * total
            C[6, i] = diag
            C[7, i] = jnp.where(inside, W / diag, 0.0)

    def sum_across(v, C, level):
        near = neighbours(v, level)
        out = []
        for i in range(G):
            out.append(
                (C[0, i] * near[0][i] + C[1, i] * near[1][i])
                + (C[2, i] * near[2][i] + C[3, i] * near[3][i])
                + (C[4, i] * near[4][i] + C[5, i] * near[5][i])
            )
        return out

    def sweep_whole(v, s, C, level):
        total = sum_across(v, C, level)
        return [(1.0 - W) * v[i] + C[7, i] * (s[i] + total[i]) for i in range(G)]

    def coarsen(v, level):
        st, zs = 1 << (level - 2), 1 << level
        rows = v[0].shape[0]
        out = []
        for i in range(G):
            E[i, pl.ds(0, rows)] = pair_lanes(pair_lanes(v[i], st), zs)
            out.append(0.125 * (E[i, pl.ds(0, rows // 2, stride=2)] + E[i, pl.ds(1, rows // 2, stride=2)]))
        return out

    def refine(v):
        rows = v[0].shape[0]
        out = []
        for i in range(G):
            E[i, pl.ds(0, rows, stride=2)] = v[i]
            E[i, pl.ds(1, rows, stride=2)] = v[i]
            out.append(E[i, pl.ds(0, 2 * rows)])
        return out

    def pair_of(level, V, S, D, coeffs, first, second, row, rows):
        one = [residual(level, V, S, D, coeffs, i, row, rows) for i in (first, second) if i is not None]
        return one[0] if len(one) == 1 else one[0] + one[1]

    setup(0, B0, CX0, CY0, CM0, CP0, Q0, D0, 2, 23, row0, rows0, H0, X0, Y0)
    first_sweep(V0, Q0, SZ0, H0, H0 + X0, HY, Y0)
    sweep(0, V0, U0, SZ0, Q0, coeffs0, H0 - 1, H0 + X0 + 1, HY - 2, Y0 + 4)
    for p in range(-1, X0 // 2 + 1):
        i = H0 + 2 * p
        SZ1[H1 + p, pl.ds(HY - 1, Y0 // 2 + 2)] = halve(
            pair_of(0, U0, SZ0, D0, coeffs0, i, i + 1, HY - 2, Y0 + 4), 1, p + 1
        )
    recv_all(beta1_halo)
    setup(1, B1, CX1, CY1, CM1, CP1, Q1, D1, 1, 17, row1, rows1, H1, X0 // 2, Y0 // 2)
    first_sweep(V1, Q1, SZ1, H1 - 1, H1 + X0 // 2 + 1, HY - 1, Y0 // 2 + 2)
    sweep(1, V1, U1, SZ1, Q1, coeffs1, H1 - 2, H1 + X0 // 2 + 2, HY - 2, Y0 // 2 + 4)
    last = X0 // 4 + 1
    planes = []
    for p in range(-2, last + 1):
        i = H1 + 2 * p
        pair = pair_of(
            1, U1, SZ1, D1, coeffs1, None if p == -2 else i, None if p == last else i + 1, HY - 4, Y0 // 2 + 8
        )
        planes.append(halve(pair, 2, p + 2))
    k = lane_of(planes[0].shape) & 3
    middle, sides = pack(planes[2:6]), pack(planes[6:8] + planes[0:2])
    PS[0, pl.ds(0, 12)] = middle
    PS[1, pl.ds(0, 12)] = sides
    Z2[g, pl.ds(6, 12)] = jnp.where(k >= 2, sides, 0.0)
    Z2[g + 1, pl.ds(6, 12)] = middle
    Z2[g + 2, pl.ds(6, 12)] = jnp.where(k < 2, sides, 0.0)
    recv_all(beta2_window)
    setup_whole([GB[i] for i in range(G)], C2, 2, 8 * b - 8, ry2)
    z2 = [Z2[i + 1] for i in range(G)]
    v = [C2[7, i] * z2[i] for i in range(G)]
    v = sweep_whole(v, z2, C2, 2)
    total = sum_across(v, C2, 2)
    for i in range(G):
        E[i, pl.ds(0, 24)] = pair_lanes(pair_lanes(z2[i] - (C2[6, i] * v[i] - total[i]), 1), 4)
        F[i + 1] = 0.125 * (E[i, pl.ds(4, 8, stride=2)] + E[i, pl.ds(5, 8, stride=2)])
    slot = (lane_of((8, LANES)) & 1) + ((lane_of((8, LANES)) >> 1) & 2)
    packed = jnp.where(slot == 2, F[g + 2], P3[...])
    packed = jnp.where(slot == 1, F[g + 1], packed)
    PG[...] = jnp.where(slot == 0, F[g], packed)
    hear(1)
    gather_start()
    recv_all(source_halo)
    part = {-1: pl.ds(0, 8), 0: pl.ds(0, 12), 1: pl.ds(4, 8)}
    source2_window = window_copies(1, lambda dy: PS.at[:, part[dy]], lambda dy: GL.at[g, 1 - dy, :, part[dy]])
    start_all(source2_window)
    GL[g, 1] = PS[...]

    land_all(beta_late)
    setup(0, B0, CX0, CY0, CM0, CP0, Q0, D0, 1, 23, row0, rows0, H0, X0, Y0)
    first_sweep(V0, Q0, S0, 1, 23, row0, rows0)
    sweep(0, V0, U0, S0, Q0, coeffs0, 2, 22, row0, rows0)
    for p in range(X0 // 2):
        i = H0 + 2 * p
        S1[H1 + p, pl.ds(HY, Y0 // 2)] = halve(pair_of(0, U0, S0, D0, coeffs0, i, i + 1, HY, Y0), 1, p)
    source1_halo = halo_copies(3, S1, X0 // 2, H1, Y0 // 2, 4, 4, 4)
    start_all(source1_halo)
    land_all(beta1_late)
    setup(1, B1, CX1, CY1, CM1, CP1, Q1, D1, 1, 17, row1, rows1, H1, X0 // 2, Y0 // 2)

    for copies in (beta_halo, beta1_halo, beta2_window, source_halo, beta_late[0], beta1_late[0]):
        sent_all(copies)
    recv_all(source1_halo)
    first_sweep(V1, Q1, S1, 1, 17, row1, rows1)
    sweep(1, V1, U1, S1, Q1, coeffs1, 2, 16, row1, rows1)
    gather_recv()
    slot = (lane_of((ry3, LANES)) & 1) + ((lane_of((ry3, LANES)) >> 1) & 2)
    parts = [GE[0, i, pl.ds(10, ry3)] + GE[1, i, pl.ds(6, ry3)] for i in range(G)]

    def spread(v):
        return pair_lanes(pair_lanes(v, 1), 4)

    beta3 = [spread(jnp.where(slot == 3, a, 0.0)) for a in parts]
    s3 = []
    for i in range(G):
        mine = jnp.where(slot == 1, parts[i], 0.0)
        if i + 1 < G:
            mine = jnp.where(slot == 0, parts[i + 1], mine)
        if i > 0:
            mine = jnp.where(slot == 2, parts[i - 1], mine)
        s3.append(spread(mine))
    setup_whole(beta3, C3, 3, 0, ry3)
    beta4 = coarsen(beta3, 3)
    setup_whole(beta4, C4, 4, 0, ry4)

    v = [C3[7, i] * s3[i] for i in range(G)]
    v = sweep_whole(v, s3, C3, 3)
    for i in range(G):
        F3[0, i] = v[i]
        F3[1, i] = s3[i]
    total = sum_across(v, C3, 3)
    s4 = coarsen([s3[i] - (C3[6, i] * v[i] - total[i]) for i in range(G)], 3)

    def dot(a, c):
        acc = a[0] * c[0]
        for i in range(1, G):
            acc = acc + a[i] * c[i]
        part = acc[0:8]
        for j in range(8, ry4, 8):
            part = part + acc[j : j + 8]
        return jnp.sum(jnp.sum(part, axis=0, keepdims=True), axis=1, keepdims=True)

    def apply(r):
        near = sum_across(r, C4, 4)
        return [C4[6, i] * r[i] - near[i] for i in range(G)]

    p, r, q = s4, s4, apply(s4)
    rr = dot(r, r)
    alpha = rr / dot(r, q)
    x4 = [alpha * p[i] for i in range(G)]
    for _ in range(COARSE - 1):
        r = [r[i] - alpha * q[i] for i in range(G)]
        w = apply(r)
        new, delta = dot(r, r), dot(r, w)
        ratio = new / rr
        alpha = new / (delta - ratio * (new / alpha))
        p = [r[i] + ratio * p[i] for i in range(G)]
        q = [w[i] + ratio * q[i] for i in range(G)]
        x4 = [x4[i] + alpha * p[i] for i in range(G)]
        rr = new

    up = refine(x4)
    s3 = [F3[1, i] for i in range(G)]
    v = [F3[0, i] + up[i] for i in range(G)]
    for _ in range(SWEEPS):
        v = sweep_whole(v, s3, C3, 3)
    for i in range(G):
        for odd in (0, 1):
            E2[i, pl.ds(8 + odd, ry3, stride=2)] = v[i]
    recv_all(source2_window)
    for j in (0, 1):
        for i in range(G):
            GS[j, i, pl.ds(10, 8)] = GL[i, 0, j, pl.ds(4, 8)]
            GS[j, i, pl.ds(22, 8)] = GL[i, 2, j, pl.ds(0, 8)]
            GS[j, i, pl.ds(14, 12)] = GS[j, i, pl.ds(14, 12)] + GL[i, 1, j, pl.ds(0, 12)]
    k = lane_of((24, LANES)) & 3
    s2 = []
    for i in range(G):
        left = GS[1, i - 1, pl.ds(8, 24)] if i > 0 else 0.0
        right = GS[1, i + 1, pl.ds(8, 24)] if i + 1 < G else 0.0
        s2.append(GS[0, i, pl.ds(8, 24)] + jnp.where(k < 2, left, right))
    v = [C2[7, i] * s2[i] for i in range(G)]
    v = sweep_whole(v, s2, C2, 2)
    v = [v[i] + E2[i, pl.ds(pl.multiple_of(b * 8, 8), 24)] for i in range(G)]
    for _ in range(SWEEPS):
        v = sweep_whole(v, s2, C2, 2)
    for i in range(G):
        V2[i + 1] = v[i]

    for x2 in range(-2, 6):
        k = x2 % 4
        window = V2[g + 1 + x2 // 4]
        one = jnp.where((lane_of(window.shape) & 3) == k, window, 0.0)
        one = one + roll(one, 1 if k in (0, 2) else -1, 1)
        one = one + roll(one, 2 if k in (0, 1) else -2, 1)
        T[x2 + 2, pl.ds(0, 24)] = one
    for x2 in range(-2, 6):
        add = T[x2 + 2, pl.ds(6, 12)]
        for i in (2 * x2 + 5, 2 * x2 + 6):
            if 2 <= i < 16:
                for odd in (0, 1):
                    at = pl.ds(row1 + odd, 12, stride=2)
                    U1[i, at] = U1[i, at] + add
    sweep(1, U1, V1, S1, Q1, coeffs1, 3, 15, row1, rows1)
    sweep(1, V1, U1, S1, Q1, coeffs1, 4, 14, row1, rows1)

    def prolong0(i, carry):
        add = U1[i + 3, pl.ds(6, 20)]
        for half in (0, 1):
            for odd in (0, 1):
                at = pl.ds(row0 + odd, 20, stride=2)
                U0[2 * i + half, at] = U0[2 * i + half, at] + add
        return carry

    lax.fori_loop(1, 11, prolong0, 0, unroll=True)
    sweep(0, U0, V0, S0, Q0, coeffs0, 3, 21, row0, rows0)
    sweep(0, V0, out_ref, S0, Q0, coeffs0, 4, 20, HY, Y0, H0, HY)

    sent_all(source1_halo)
    sent_all(source2_window)
    gather_sent()


def in_one_kernel(G, B, right_side, beta):
    level0 = pltpu.VMEM((X0 + 2 * H0, Y0 + 2 * HY, LANES), F32)
    level1 = pltpu.VMEM((X0 // 2 + 2 * H1, Y0 // 2 + 2 * HY, LANES), F32)
    return pl.pallas_call(
        functools.partial(kernel, G, B),
        out_shape=jax.ShapeDtypeStruct(right_side.shape, F32),
        in_specs=[pl.BlockSpec(memory_space=pltpu.HBM)] * 2,
        out_specs=pl.BlockSpec(memory_space=pltpu.VMEM),
        scratch_shapes=[level0] * 10
        + [level1] * 10
        + [
            pltpu.VMEM((12, Y0 + 8, LANES), F32),
            level0,
            level1,
            pltpu.VMEM((8, LANES), F32),
            pltpu.VMEM((2, 16, LANES), F32),
            pltpu.VMEM((8, LANES), F32),
            pltpu.VMEM((8, LANES), F32),
            pltpu.VMEM((G, 24, LANES), F32),
            pltpu.VMEM((2, G, 40, LANES), F32),
            pltpu.VMEM((G, 3, 2, 16, LANES), F32),
            pltpu.VMEM((2, G, 4 * B + 16, LANES), F32),
            pltpu.VMEM((G + 2, 24, LANES), F32),
            pltpu.VMEM((G + 2, 24, LANES), F32),
            pltpu.VMEM((8, G, 24, LANES), F32),
            pltpu.VMEM((8, G, 4 * B, LANES), F32),
            pltpu.VMEM((8, G, 2 * B, LANES), F32),
            pltpu.VMEM((G, 8 * B, LANES), F32),
            pltpu.VMEM((G, 8 * B + 16, LANES), F32),
            pltpu.VMEM((G + 2, 8, LANES), F32),
            pltpu.VMEM((2, G, 4 * B, LANES), F32),
            pltpu.VMEM((2, 2, Y0, LANES), F32),
            pltpu.VMEM((2, X0, 8, LANES), F32),
            pltpu.VMEM((2, 2, Y0 // 2, LANES), F32),
            pltpu.VMEM((2, X0 // 2, 8, LANES), F32),
            pltpu.SemaphoreType.DMA((4, 8)),
            pltpu.SemaphoreType.DMA((4, 8)),
            pltpu.SemaphoreType.DMA((2, 4)),
            pltpu.SemaphoreType.DMA((2, 4)),
            pltpu.SemaphoreType.DMA((2, 3 * G)),
            pltpu.SemaphoreType.DMA((2, 3 * G)),
            pltpu.SemaphoreType.DMA((1,)),
            pltpu.SemaphoreType.DMA((1,)),
            pltpu.SemaphoreType.REGULAR((2,)),
            pltpu.SemaphoreType.DMA((3,)),
        ],
        compiler_params=pltpu.CompilerParams(
            collective_id=0, has_side_effects=True, vmem_limit_bytes=40 * 1024 * 1024
        ),
    )(*(pltpu.with_memory_space_constraint(a, pltpu.HBM) for a in (right_side, beta)))


relax_weight = 2.0 / 3.0


def with_halo(shard, sides, width):
    for axis, dim in sides:
        size, length = (lax.axis_size(axis), shard.shape[dim])
        up = [(i, (i + 1) % size) for i in range(size - 1)]
        down = [(j, i) for i, j in up]
        last = lax.slice_in_dim(shard, length - width, length, axis=dim)
        leading = lax.slice_in_dim(shard, 0, width, axis=dim)
        before = lax.ppermute(last, axis, up)
        after = lax.ppermute(leading, axis, down)
        shard = jnp.concatenate([before, shard, after], axis=dim)
    return shard


def from_partner(block, axis, apart):
    count = lax.axis_size(axis)
    route = []
    for low in range(count):
        high = low | 1 << apart
        if high != low and high < count:
            route += [(low, high), (high, low)]
    return lax.ppermute(block, axis, route)


def pad_zeros(field):
    return jnp.pad(field, 1)


def pad_local(field):
    extended = with_halo(field, (("grp", 0), ("box", 1)), 1)
    return jnp.pad(extended, ((0, 0), (0, 0), (1, 1)))


def face_coeffs(padded_beta):
    face_x = 0.5 * (padded_beta[1:, 1:-1, 1:-1] + padded_beta[:-1, 1:-1, 1:-1])
    face_y = 0.5 * (padded_beta[1:-1, 1:, 1:-1] + padded_beta[1:-1, :-1, 1:-1])
    face_z = 0.5 * (padded_beta[1:-1, 1:-1, 1:] + padded_beta[1:-1, 1:-1, :-1])
    return (face_x, face_y, face_z)


def inverse_diagonal(coeffs, scale):
    face_x, face_y, face_z = coeffs
    total = (
        face_x[:-1]
        + face_x[1:]
        + face_y[:, :-1]
        + face_y[:, 1:]
        + face_z[:, :, :-1]
        + face_z[:, :, 1:]
    )
    return 1.0 / (scale * total)


def apply_operator(padded, coeffs, scale):
    face_x, face_y, face_z = coeffs
    centre = padded[1:-1, 1:-1, 1:-1]
    total = face_x[:-1] * (centre - padded[:-2, 1:-1, 1:-1]) + face_x[1:] * (
        centre - padded[2:, 1:-1, 1:-1]
    )
    total = (
        total
        + face_y[:, :-1] * (centre - padded[1:-1, :-2, 1:-1])
        + face_y[:, 1:] * (centre - padded[1:-1, 2:, 1:-1])
    )
    total = (
        total
        + face_z[:, :, :-1] * (centre - padded[1:-1, 1:-1, :-2])
        + face_z[:, :, 1:] * (centre - padded[1:-1, 1:-1, 2:])
    )
    return scale * total


def jacobi_sweeps(field, source, coeffs, inverse, scale, count, padder):
    for sweep_index in range(count):
        field = (
            field + relax_weight * (source - apply_operator(padder(field), coeffs, scale)) * inverse
        )
    return field


def conjugate_solve(source, coeffs, scale, count):
    field = jnp.zeros_like(source)
    remain = source
    direction = source
    norm_now = jnp.sum(remain * remain)
    for step_index in range(count):
        image = apply_operator(pad_zeros(direction), coeffs, scale)
        alpha = norm_now / jnp.sum(direction * image)
        field = field + alpha * direction
        remain = remain - alpha * image
        norm_next = jnp.sum(remain * remain)
        direction = remain + norm_next / norm_now * direction
        norm_now = norm_next
    return field


def restrict_mean(field):
    size_a, size_b, size_c = field.shape
    blocks = field.reshape(size_a // 2, 2, size_b // 2, 2, size_c // 2, 2)
    return jnp.mean(blocks, axis=(1, 3, 5))


def prolong_copy(field):
    return jnp.repeat(jnp.repeat(jnp.repeat(field, 2, axis=0), 2, axis=1), 2, axis=2)


def merge_groups(pieces):
    group_index = lax.axis_index("grp")
    for bit_index in range(lax.axis_size("grp").bit_length() - 1):
        partner = from_partner(pieces, "grp", bit_index)
        upper = group_index >> bit_index & 1 == 1
        pieces = tuple(
            (
                jnp.where(
                    upper,
                    jnp.concatenate([theirs, own_piece], 0),
                    jnp.concatenate([own_piece, theirs], 0),
                )
                for own_piece, theirs in zip(pieces, partner)
            )
        )
    return pieces


def merge_boxes(pieces):
    return lax.all_gather(pieces, "box", axis=1, tiled=True)


def shards(right_side, beta):
    source = right_side
    level_beta = beta
    saved = []
    for level in range(LEVELS):
        scale = 0.25**level
        coeffs = face_coeffs(pad_local(level_beta))
        inverse = inverse_diagonal(coeffs, scale)
        field = relax_weight * source * inverse
        field = jacobi_sweeps(field, source, coeffs, inverse, scale, SWEEPS - 1, pad_local)
        residual = source - apply_operator(pad_local(field), coeffs, scale)
        saved.append((field, source, coeffs, inverse, scale))
        source = restrict_mean(residual)
        level_beta = restrict_mean(level_beta)
    low_scale = 0.25**LEVELS
    whole_source, whole_beta = merge_boxes(merge_groups((source, level_beta)))
    low_coeffs = face_coeffs(pad_zeros(whole_beta))
    whole_field = conjugate_solve(whole_source, low_coeffs, low_scale, COARSE)
    block_a, block_b, block_c = source.shape
    field = lax.dynamic_slice(
        whole_field,
        (lax.axis_index("grp") * block_a, lax.axis_index("box") * block_b, 0),
        (block_a, block_b, block_c),
    )
    for level in range(LEVELS - 1, -1, -1):
        kept, level_source, coeffs, inverse, scale = saved[level]
        field = kept + prolong_copy(field)
        field = jacobi_sweeps(field, level_source, coeffs, inverse, scale, SWEEPS, pad_local)
    return field


def solution(mesh):
    placed = P("grp", "box", None)
    G, B = mesh.shape["grp"], mesh.shape["box"]
    small = (G, B) in ((4, 8), (8, 8), (4, 16), (8, 4), (2, 16))

    def local(right_side, beta):
        if small and right_side.shape == (X0, Y0, LANES):
            return in_one_kernel(G, B, right_side, beta)
        return shards(right_side, beta)

    return jax.shard_map(local, mesh=mesh, in_specs=(placed, placed), out_specs=placed, check_vma=False)
```

```python
import functools

import jax
import jax.numpy as jnp
from jax import lax
from jax.experimental import pallas as pl
from jax.experimental.pallas import tpu as pltpu
from jax.sharding import PartitionSpec as P

LEVELS = 4
SWEEPS = 2
COARSE = 8
W = 2.0 / 3.0
MESH = pl.DeviceIdType.MESH
F32 = jnp.float32

X0, Y0, LANES = 16, 32, 128
H0 = 4
H1 = 5
HY = 8
DIRS = [(dx, dy) for dx in (-1, 0, 1) for dy in (-1, 0, 1) if (dx, dy) != (0, 0)]


def roll(v, shift, axis):
    return pltpu.roll(v, shift % v.shape[axis], axis)


def lane_of(shape):
    return lax.broadcasted_iota(jnp.int32, shape, len(shape) - 1)


def pair_lanes(v, apart):
    lane = lane_of(v.shape)
    return v + jnp.where((lane & apart) == 0, roll(v, -apart, 1), roll(v, apart, 1))


def span(size, halo, step, near, far):
    if step == 0:
        return (halo, size), (halo, size)
    if step < 0:
        return (halo + near, far - near), (halo + size + near, far - near)
    return (halo + size - far, far - near), (halo - far, far - near)


def kernel(
    G, B, rs_ref, be_ref, out_ref,
    B0, S0, V0, U0, CX0, CY0, CM0, CP0, Q0,
    B1, S1, V1, U1, CX1, CY1, CM1, CP1, Q1,
    T, SZ0, SZ1, PB, PS, P3, PG, GB, GS, GL, GE, V2, Z2, C2, C3, C4, E, E2, F, F3, LX0, LY0, LX1, LY1,
    halo_send, halo_recv, late_send, late_recv, win_send, win_recv, ga_send, ga_recv, rounds, loc_sem,
):
    n = G * B
    g = lax.axis_index("grp")
    b = lax.axis_index("box")
    me = g * B + b
    ry2, ry3, ry4 = 8 * B, 4 * B, 2 * B

    own0 = (pl.ds(H0, X0), pl.ds(HY, Y0))
    load_b = pltpu.make_async_copy(be_ref, B0.at[own0[0], own0[1]], loc_sem.at[0])
    load_s = pltpu.make_async_copy(rs_ref, S0.at[own0[0], own0[1]], loc_sem.at[1])
    load_b.start()
    load_s.start()
    load_z = pltpu.make_async_copy(rs_ref, SZ0.at[own0[0], own0[1]], loc_sem.at[2])
    load_z.start()

    barrier = pltpu.get_barrier_semaphore()

    expected = 0
    for dx, dy in DIRS:
        there = (g + dx >= 0) & (g + dx < G) & (b + dy >= 0) & (b + dy < B)
        expected = expected + there.astype(jnp.int32)

        @pl.when(there)
        def _():
            pl.semaphore_signal(barrier, inc=1, device_id=(g + dx, b + dy), device_id_type=MESH)

    reach = max(1, -(-(B - 2) // 3))
    others = []
    for far in range(2, G):
        for dx in (-far, far):
            others += [(dx, dy) for dy in (-1, 0, 1)]
    for far in range(2, reach + 1):
        others += [(0, -far), (0, far)]
    for dx, dy in others:
        there = (g + dx >= 0) & (g + dx < G) & (b + dy >= 0) & (b + dy < B)
        expected = expected + there.astype(jnp.int32)

        @pl.when(there)
        def _():
            pl.semaphore_signal(barrier, inc=1, device_id=(g + dx, b + dy), device_id_type=MESH)

    def boxes_of(k):
        for far in range(k * reach + 1, (k + 1) * reach + 1):
            for dy in (-far, far):
                yield b + dy, (b + dy >= 0) & (b + dy < B)

    def tell(k):
        for other, there in boxes_of(k):

            @pl.when(there)
            def _():
                pl.semaphore_signal(rounds.at[k], inc=1, device_id=(g, other), device_id_type=MESH)

    def hear(k):
        count = 0
        for _, there in boxes_of(k):
            count = count + there.astype(jnp.int32)
        pl.semaphore_wait(rounds.at[k], count)

    for ref, nx, hx, ny in ((B0, X0, H0, Y0), (S0, X0, H0, Y0), (B1, X0 // 2, H1, Y0 // 2), (S1, X0 // 2, H1, Y0 // 2)):
        rows = ny + 2 * HY
        planes = nx + 2 * hx

        @pl.when(g == 0)
        def _():
            ref[pl.ds(0, hx)] = jnp.zeros((hx, rows, LANES), F32)

        @pl.when(g == G - 1)
        def _():
            ref[pl.ds(hx + nx, hx)] = jnp.zeros((hx, rows, LANES), F32)

        @pl.when(b == 0)
        def _():
            ref[:, pl.ds(0, HY)] = jnp.zeros((planes, HY, LANES), F32)

        @pl.when(b == B - 1)
        def _():
            ref[:, pl.ds(HY + ny, HY)] = jnp.zeros((planes, HY, LANES), F32)

    load_b.wait()

    def halve(pair, apart, slot):
        rows = pair.shape[0]
        T[slot, pl.ds(0, rows)] = pair_lanes(pair, apart)
        return 0.125 * (T[slot, pl.ds(0, rows // 2, stride=2)] + T[slot, pl.ds(1, rows // 2, stride=2)])

    def pack(planes):
        lane = lane_of(planes[0].shape) & 3
        packed = planes[3]
        for k in (2, 1, 0):
            packed = jnp.where(lane == k, planes[k], packed)
        return packed

    for p in range(X0 // 2):
        B1[H1 + p, pl.ds(HY, Y0 // 2)] = halve(
            B0[H0 + 2 * p, pl.ds(HY, Y0)] + B0[H0 + 2 * p + 1, pl.ds(HY, Y0)], 1, p
        )
    PB[...] = pack([
        halve(B1[H1 + 2 * p, pl.ds(HY, Y0 // 2)] + B1[H1 + 2 * p + 1, pl.ds(HY, Y0 // 2)], 2, p)
        for p in range(X0 // 4)
    ])
    GB[g, pl.ds(8, 8)] = PB[...]
    T[0, pl.ds(0, 8)] = pair_lanes(pair_lanes(PB[...], 1), 4)
    P3[...] = jnp.zeros((8, LANES), F32)
    P3[pl.ds(2, 4)] = 0.125 * (T[0, pl.ds(0, 4, stride=2)] + T[0, pl.ds(1, 4, stride=2)])

    load_s.wait()
    load_z.wait()
    pl.semaphore_wait(barrier, expected)

    def there_from(dx, dy):
        return (g + dx >= 0) & (g + dx < G) & (b + dy >= 0) & (b + dy < B)

    def halo_copies(kind, ref, nx, hx, ny, deep, tall, corner):
        made = []
        for at, (dx, dy) in enumerate(DIRS):
            (sx, lx), (tx, _) = span(nx, hx, dx, 0, deep if dy == 0 else corner)
            (sy, ly), (ty, _) = span(ny, HY, dy, 0, tall if dx == 0 else corner)
            copy = pltpu.make_async_remote_copy(
                src_ref=ref.at[pl.ds(sx, lx), pl.ds(sy, ly)],
                dst_ref=ref.at[pl.ds(tx, lx), pl.ds(ty, ly)],
                send_sem=halo_send.at[kind, at],
                recv_sem=halo_recv.at[kind, at],
                device_id=(g + dx, b + dy),
                device_id_type=MESH,
            )
            made.append((copy, there_from(dx, dy), there_from(-dx, -dy)))
        return made

    def late_copies(kind, ref, LX, LY, nx, hx, ny, near, far):
        made, land = [], []
        for at, (dx, dy) in enumerate(((-1, 0), (1, 0), (0, -1), (0, 1))):
            (sx, lx), (tx, _) = span(nx, hx, dx, near, far)
            (sy, ly), (ty, _) = span(ny, HY, dy, near, far)
            box = LX.at[at] if dy == 0 else LY.at[at - 2, :, pl.ds(0, far - near)]
            copy = pltpu.make_async_remote_copy(
                src_ref=ref.at[pl.ds(sx, lx), pl.ds(sy, ly)],
                dst_ref=box,
                send_sem=late_send.at[kind, at],
                recv_sem=late_recv.at[kind, at],
                device_id=(g + dx, b + dy),
                device_id_type=MESH,
            )
            here = there_from(-dx, -dy)
            made.append((copy, there_from(dx, dy), here))

            def put(tx=tx, lx=lx, ty=ty, ly=ly, box=box):
                ref[pl.ds(tx, lx), pl.ds(ty, ly)] = box[...]

            land.append((here, put))
        return made, land

    def land_all(late):
        made, land = late
        for (copy, _, here), (_, put) in zip(made, land):

            @pl.when(here)
            def _():
                copy.wait_recv()
                put()

    def start_all(copies):
        for copy, there, _ in copies:
            pl.when(there)(copy.start)

    def recv_all(copies):
        for copy, _, here in copies:
            pl.when(here)(copy.wait_recv)

    def sent_all(copies):
        for copy, there, _ in copies:
            pl.when(there)(copy.wait_send)

    def window_copies(kind, packed, spot):
        made = []
        for o in range(G):
            for dy in (-1, 0, 1):
                if (o, dy) == (0, 0):
                    continue
                at = 3 * o + dy + 1
                copy = pltpu.make_async_remote_copy(
                    src_ref=packed(dy),
                    dst_ref=spot(dy),
                    send_sem=win_send.at[kind, at],
                    recv_sem=win_recv.at[kind, at],
                    device_id=((g + o) % G, b + dy),
                    device_id_type=MESH,
                )
                made.append((copy, (b + dy >= 0) & (b + dy < B), (b - dy >= 0) & (b - dy < B)))
        return made

    def gather_start():
        spot = GE.at[b % 2, g, pl.ds(pl.multiple_of(8 + 8 * (b // 2), 8), 8)]
        pltpu.make_async_copy(PG, spot, ga_recv.at[0]).start()

        def one(d, carry):
            peer = (me + d) % n
            pltpu.make_async_remote_copy(
                src_ref=PG,
                dst_ref=spot,
                send_sem=ga_send.at[0],
                recv_sem=ga_recv.at[0],
                device_id=(peer // B, peer % B),
                device_id_type=MESH,
            ).start()
            return carry

        lax.fori_loop(1, n, one, 0, unroll=True)

    def gather_recv():
        whole = GE.at[:, :, pl.ds(8, ry3)]
        pltpu.make_async_copy(whole, whole, ga_recv.at[0]).wait()

    def gather_sent():
        room = CX0.at[pl.ds(0, 8), pl.ds(0, n - 1)]
        pltpu.make_async_copy(room, room, ga_send.at[0]).wait()

    beta_halo = halo_copies(0, B0, X0, H0, Y0, 2, 2, 3)
    source_halo = halo_copies(1, S0, X0, H0, Y0, 3, 3, 2)
    beta1_halo = halo_copies(2, B1, X0 // 2, H1, Y0 // 2, 3, 3, 5)
    beta2_window = window_copies(0, lambda dy: PB, lambda dy: GB.at[g, pl.ds(8 - 8 * dy, 8)])
    beta_late = late_copies(0, B0, LX0, LY0, X0, H0, Y0, 2, 4)
    beta1_late = late_copies(1, B1, LX1, LY1, X0 // 2, H1, Y0 // 2, 3, 5)
    start_all(beta_halo)

    for ref in (SZ1, V1, U1, V2, Z2, GS):
        ref[...] = jnp.zeros(ref.shape, F32)
    for ref, deep in ((SZ0, 2), (V0, 2), (U0, 3)):
        for x in (H0 - deep, H0 + X0 + deep - 2):
            ref[pl.ds(x, 2)] = jnp.zeros((2, Y0 + 2 * HY, LANES), F32)
        for y in (0, HY + Y0):
            ref[pl.ds(H0 - 1, X0 + 2), pl.ds(y, HY)] = jnp.zeros((X0 + 2, HY, LANES), F32)
    for ref, nx, hx, ny, near in ((B0, X0, H0, Y0, 2), (B1, X0 // 2, H1, Y0 // 2, 3)):
        for x in (hx - near - 2, hx + nx + near):
            ref[pl.ds(x, 2), pl.ds(HY, ny)] = jnp.zeros((2, ny, LANES), F32)
        for y in (HY - near - 2, HY + ny + near):
            ref[pl.ds(hx, nx), pl.ds(y, 2)] = jnp.zeros((nx, 2, LANES), F32)
    CX1[X0 // 2 + 2 * H1 - 1] = jnp.zeros((Y0 // 2 + 2 * HY, LANES), F32)
    CY1[:, pl.ds(HY + Y0 // 2 + 4, 4)] = jnp.zeros((X0 // 2 + 2 * H1, 4, LANES), F32)
    for side, edge in ((0, 0), (2, B - 1)):

        @pl.when(b == edge)
        def _():
            GB[:, pl.ds(8 * side, 8)] = jnp.zeros((G, 8, LANES), F32)
            GL[:, side] = jnp.zeros((G, 2, 16, LANES), F32)

    E2[:, pl.ds(0, 8)] = jnp.zeros((G, 8, LANES), F32)
    E2[:, pl.ds(8 + ry2, 8)] = jnp.zeros((G, 8, LANES), F32)
    F[0] = jnp.zeros((8, LANES), F32)
    F[G + 1] = jnp.zeros((8, LANES), F32)
    GE[:, :, pl.ds(0, 8)] = jnp.zeros((2, G, 8, LANES), F32)
    GE[:, :, pl.ds(8 + ry3, 8)] = jnp.zeros((2, G, 8, LANES), F32)

    start_all(beta1_halo)
    start_all(beta2_window)
    tell(0)

    def setup(level, Bl, CX, CY, CM, CP, Q, first, last, row, rows, hx, nx, ny):
        apart = 1 << level
        h = 0.5 * 0.25**level

        def plane(i, carry):
            at = pl.ds(row, rows)
            c = Bl[i, at]
            xm = Bl[i - 1, at]
            xp = Bl[i + 1, at]
            ym = Bl[i, pl.ds(row - 1, rows)]
            yp = Bl[i, pl.ds(row + 1, rows)]
            lane = lane_of(c.shape)
            low = lane >= apart
            high = lane < LANES - apart
            zm = jnp.where(low, roll(c, apart, 1), 0.0)
            zp = jnp.where(high, roll(c, -apart, 1), 0.0)
            CX[i, at] = h * (c + xm)
            CY[i, at] = h * (c + ym)
            CM[i, at] = jnp.where(low, h * (c + zm), 0.0)
            CP[i, at] = jnp.where(high, h * (c + zp), 0.0)
            d = h * (6.0 * c + ((xm + xp) + (ym + yp) + (zm + zp)))
            x = g * nx + i - hx
            y = lax.broadcasted_iota(jnp.int32, c.shape, 0) + (b * ny + row - HY)
            inside = (y >= 0) & (y < B * ny) & (x >= 0) & (x < G * nx)
            Q[i, at] = jnp.where(inside, W / d, 0.0)
            return carry

        lax.fori_loop(first, last, plane, 0, unroll=True)

    def across(level, V, CX, CY, CM, CP, i, row, rows):
        apart = 1 << level
        at = pl.ds(row, rows)
        up = pl.ds(row + 1, rows)
        v = V[i, at]
        total = CX[i, at] * V[i - 1, at] + CX[i + 1, at] * V[i + 1, at]
        total = total + (CY[i, at] * V[i, pl.ds(row - 1, rows)] + CY[i, up] * V[i, up])
        total = total + (CM[i, at] * roll(v, apart, 1) + CP[i, at] * roll(v, -apart, 1))
        return v, total

    def first_sweep(V, Q, S, first, last, row, rows):
        def plane(i, carry):
            V[i, pl.ds(row, rows)] = Q[i, pl.ds(row, rows)] * S[i, pl.ds(row, rows)]
            return carry

        lax.fori_loop(first, last, plane, 0, unroll=True)

    def sweep(level, V, U, S, Q, coeffs, first, last, row, rows, drop_x=0, drop_y=0):
        def plane(i, carry):
            v, total = across(level, V, *coeffs, i, row, rows)
            U[i - drop_x, pl.ds(row - drop_y, rows)] = (1.0 - W) * v + Q[i, pl.ds(row, rows)] * (
                S[i, pl.ds(row, rows)] + total
            )
            return carry

        lax.fori_loop(first, last, plane, 0, unroll=True)

    coeffs0 = (CX0, CY0, CM0, CP0)
    coeffs1 = (CX1, CY1, CM1, CP1)
    row0, rows0 = 4, 40
    row1, rows1 = 4, 24

    recv_all(beta_halo)
    hear(0)
    tell(1)
    start_all(source_halo)
    start_all(beta_late[0])
    start_all(beta1_late[0])
    def neighbours(v, level):
        st, zs = 1 << (level - 2), 1 << level
        before = [v[i - 1] for i in range(G)]
        after = [v[(i + 1) % G] for i in range(G)]
        if st == 4:
            xm, xp = before, after
        else:
            k = lane_of(v[0].shape) & 3
            xm = [jnp.where(k >= st, roll(v[i], st, 1), roll(before[i], st - 4, 1)) for i in range(G)]
            xp = [jnp.where(k < 4 - st, roll(v[i], -st, 1), roll(after[i], 4 - st, 1)) for i in range(G)]
        ym = [roll(a, 1, 0) for a in v]
        yp = [roll(a, -1, 0) for a in v]
        zm = [roll(a, zs, 1) for a in v]
        zp = [roll(a, -zs, 1) for a in v]
        return xm, xp, ym, yp, zm, zp

    def setup_whole(beta, C, level, first, total_rows):
        st, zs = 1 << (level - 2), 1 << level
        h = 0.5 * 0.25**level
        near = neighbours(beta, level)
        shape = beta[0].shape
        lane = lane_of(shape)
        row = lax.broadcasted_iota(jnp.int32, shape, 0) + first
        inside = (row >= 0) & (row < total_rows)
        for i in range(G):
            ok = [
                inside & ((lane & 3) >= st) if i == 0 else inside,
                inside & ((lane & 3) < 4 - st) if i == G - 1 else inside,
                (row > 0) & (row < total_rows),
                (row >= 0) & (row < total_rows - 1),
                inside & (lane >= zs),
                inside & (lane < LANES - zs),
            ]
            total = 6.0 * beta[i]
            for d in range(6):
                there = jnp.where(ok[d], near[d][i], 0.0)
                total = total + there
                C[d, i] = jnp.where(ok[d], h * (beta[i] + there), 0.0)
            diag = h * total
            C[6, i] = diag
            C[7, i] = jnp.where(inside, W / diag, 0.0)

    def sum_across(v, C, level):
        near = neighbours(v, level)
        out = []
        for i in range(G):
            out.append(
                (C[0, i] * near[0][i] + C[1, i] * near[1][i])
                + (C[2, i] * near[2][i] + C[3, i] * near[3][i])
                + (C[4, i] * near[4][i] + C[5, i] * near[5][i])
            )
        return out

    def sweep_whole(v, s, C, level):
        total = sum_across(v, C, level)
        return [(1.0 - W) * v[i] + C[7, i] * (s[i] + total[i]) for i in range(G)]

    def coarsen(v, level):
        st, zs = 1 << (level - 2), 1 << level
        rows = v[0].shape[0]
        out = []
        for i in range(G):
            E[i, pl.ds(0, rows)] = pair_lanes(pair_lanes(v[i], st), zs)
            out.append(0.125 * (E[i, pl.ds(0, rows // 2, stride=2)] + E[i, pl.ds(1, rows // 2, stride=2)]))
        return out

    def refine(v):
        rows = v[0].shape[0]
        out = []
        for i in range(G):
            E[i, pl.ds(0, rows, stride=2)] = v[i]
            E[i, pl.ds(1, rows, stride=2)] = v[i]
            out.append(E[i, pl.ds(0, 2 * rows)])
        return out

    def fluxes(level, V, S, Bl, coeffs, i, row, rows, slot):
        CX, CY, CM, _ = coeffs
        apart = 1 << level
        at, more, less = pl.ds(row, rows), pl.ds(row, rows + 1), pl.ds(row - 1, rows + 1)
        v, w = V[i, at], V[i + 1, at]
        lane = lane_of(v.shape)
        edge = (lane < apart) | (lane >= LANES - apart)
        wall = jnp.where(edge, (0.5 * 0.25**level) * (Bl[i, at] * v + Bl[i + 1, at] * w), 0.0)
        T[slot, pl.ds(0, rows)] = (S[i, at] + S[i + 1, at]) - (
            CX[i, at] * (v - V[i - 1, at]) + CX[i + 2, at] * (w - V[i + 2, at]) + wall
        )
        T[slot + 12, pl.ds(0, rows + 1)] = CY[i, more] * (V[i, more] - V[i, less]) + CY[i + 1, more] * (
            V[i + 1, more] - V[i + 1, less]
        )
        T[slot + 24, pl.ds(0, rows)] = CM[i, at] * (v - roll(v, apart, 1)) + CM[i + 1, at] * (w - roll(w, apart, 1))

    def restricted(level, half, slot):
        apart = 1 << level

        def every(k, first):
            return T[k, pl.ds(first, half, stride=2)]

        total = (every(slot, 0) + every(slot, 1)) - (every(slot + 12, 0) - every(slot + 12, 2))
        z = every(slot + 24, 0) + every(slot + 24, 1)
        z = jnp.where((lane_of(z.shape) & apart) == 0, z - roll(z, -2 * apart, 1), 0.0)
        return 0.125 * pair_lanes(total - z, apart)

    setup(0, B0, CX0, CY0, CM0, CP0, Q0, 2, 23, row0, rows0, H0, X0, Y0)
    first_sweep(V0, Q0, SZ0, H0, H0 + X0, HY, Y0)
    sweep(0, V0, U0, SZ0, Q0, coeffs0, H0 - 1, H0 + X0 + 1, HY - 2, Y0 + 4)
    for p in range(-1, X0 // 2 + 1):
        fluxes(0, U0, SZ0, B0, coeffs0, H0 + 2 * p, HY - 2, Y0 + 4, p + 1)
    for p in range(-1, X0 // 2 + 1):
        SZ1[H1 + p, pl.ds(HY - 1, Y0 // 2 + 2)] = restricted(0, Y0 // 2 + 2, p + 1)
    recv_all(beta1_halo)
    setup(1, B1, CX1, CY1, CM1, CP1, Q1, 1, 17, row1, rows1, H1, X0 // 2, Y0 // 2)
    first_sweep(V1, Q1, SZ1, H1 - 1, H1 + X0 // 2 + 1, HY - 1, Y0 // 2 + 2)
    sweep(1, V1, U1, SZ1, Q1, coeffs1, H1 - 2, H1 + X0 // 2 + 2, HY - 2, Y0 // 2 + 4)
    last = X0 // 4 + 1
    planes = []
    for p in range(-2, last + 1):
        fluxes(1, U1, SZ1, B1, coeffs1, H1 + 2 * p, HY - 4, Y0 // 2 + 8, p + 2)
    for p in range(-2, last + 1):
        planes.append(restricted(1, Y0 // 4 + 4, p + 2))
    k = lane_of(planes[0].shape) & 3
    middle, sides = pack(planes[2:6]), pack(planes[6:8] + planes[0:2])
    PS[0, pl.ds(0, 12)] = middle
    PS[1, pl.ds(0, 12)] = sides
    Z2[g, pl.ds(6, 12)] = jnp.where(k >= 2, sides, 0.0)
    Z2[g + 1, pl.ds(6, 12)] = middle
    Z2[g + 2, pl.ds(6, 12)] = jnp.where(k < 2, sides, 0.0)
    recv_all(beta2_window)
    setup_whole([GB[i] for i in range(G)], C2, 2, 8 * b - 8, ry2)
    z2 = [Z2[i + 1] for i in range(G)]
    v = [C2[7, i] * z2[i] for i in range(G)]
    v = sweep_whole(v, z2, C2, 2)
    total = sum_across(v, C2, 2)
    for i in range(G):
        E[i, pl.ds(0, 24)] = pair_lanes(pair_lanes(z2[i] - (C2[6, i] * v[i] - total[i]), 1), 4)
        F[i + 1] = 0.125 * (E[i, pl.ds(4, 8, stride=2)] + E[i, pl.ds(5, 8, stride=2)])
    slot = (lane_of((8, LANES)) & 1) + ((lane_of((8, LANES)) >> 1) & 2)
    packed = jnp.where(slot == 2, F[g + 2], P3[...])
    packed = jnp.where(slot == 1, F[g + 1], packed)
    PG[...] = jnp.where(slot == 0, F[g], packed)
    hear(1)
    gather_start()
    recv_all(source_halo)
    part = {-1: pl.ds(0, 8), 0: pl.ds(0, 12), 1: pl.ds(4, 8)}
    source2_window = window_copies(1, lambda dy: PS.at[:, part[dy]], lambda dy: GL.at[g, 1 - dy, :, part[dy]])
    start_all(source2_window)
    GL[g, 1] = PS[...]

    land_all(beta_late)
    setup(0, B0, CX0, CY0, CM0, CP0, Q0, 1, 23, row0, rows0, H0, X0, Y0)
    first_sweep(V0, Q0, S0, 1, 23, row0, rows0)
    sweep(0, V0, U0, S0, Q0, coeffs0, 2, 22, row0, rows0)
    for p in range(X0 // 2):
        fluxes(0, U0, S0, B0, coeffs0, H0 + 2 * p, HY, Y0, p)
    for p in range(X0 // 2):
        S1[H1 + p, pl.ds(HY, Y0 // 2)] = restricted(0, Y0 // 2, p)
    source1_halo = halo_copies(3, S1, X0 // 2, H1, Y0 // 2, 4, 4, 4)
    start_all(source1_halo)
    land_all(beta1_late)
    setup(1, B1, CX1, CY1, CM1, CP1, Q1, 1, 17, row1, rows1, H1, X0 // 2, Y0 // 2)

    for copies in (beta_halo, beta1_halo, beta2_window, source_halo, beta_late[0], beta1_late[0]):
        sent_all(copies)
    recv_all(source1_halo)
    first_sweep(V1, Q1, S1, 1, 17, row1, rows1)
    sweep(1, V1, U1, S1, Q1, coeffs1, 2, 16, row1, rows1)
    gather_recv()
    slot = (lane_of((ry3, LANES)) & 1) + ((lane_of((ry3, LANES)) >> 1) & 2)
    parts = [GE[0, i, pl.ds(10, ry3)] + GE[1, i, pl.ds(6, ry3)] for i in range(G)]

    def spread(v):
        return pair_lanes(pair_lanes(v, 1), 4)

    beta3 = [spread(jnp.where(slot == 3, a, 0.0)) for a in parts]
    s3 = []
    for i in range(G):
        mine = jnp.where(slot == 1, parts[i], 0.0)
        if i + 1 < G:
            mine = jnp.where(slot == 0, parts[i + 1], mine)
        if i > 0:
            mine = jnp.where(slot == 2, parts[i - 1], mine)
        s3.append(spread(mine))
    setup_whole(beta3, C3, 3, 0, ry3)
    beta4 = coarsen(beta3, 3)
    setup_whole(beta4, C4, 4, 0, ry4)

    v = [C3[7, i] * s3[i] for i in range(G)]
    v = sweep_whole(v, s3, C3, 3)
    for i in range(G):
        F3[0, i] = v[i]
        F3[1, i] = s3[i]
    total = sum_across(v, C3, 3)
    s4 = coarsen([s3[i] - (C3[6, i] * v[i] - total[i]) for i in range(G)], 3)

    def dot(a, c):
        acc = a[0] * c[0]
        for i in range(1, G):
            acc = acc + a[i] * c[i]
        part = acc[0:8]
        for j in range(8, ry4, 8):
            part = part + acc[j : j + 8]
        return jnp.sum(jnp.sum(part, axis=0, keepdims=True), axis=1, keepdims=True)

    def apply(r):
        near = sum_across(r, C4, 4)
        return [C4[6, i] * r[i] - near[i] for i in range(G)]

    p, r, q = s4, s4, apply(s4)
    rr = dot(r, r)
    alpha = rr / dot(r, q)
    x4 = [alpha * p[i] for i in range(G)]
    for _ in range(COARSE - 1):
        r = [r[i] - alpha * q[i] for i in range(G)]
        w = apply(r)
        new, delta = dot(r, r), dot(r, w)
        ratio = new / rr
        alpha = new / (delta - ratio * (new / alpha))
        p = [r[i] + ratio * p[i] for i in range(G)]
        q = [w[i] + ratio * q[i] for i in range(G)]
        x4 = [x4[i] + alpha * p[i] for i in range(G)]
        rr = new

    up = refine(x4)
    s3 = [F3[1, i] for i in range(G)]
    v = [F3[0, i] + up[i] for i in range(G)]
    for _ in range(SWEEPS):
        v = sweep_whole(v, s3, C3, 3)
    for i in range(G):
        for odd in (0, 1):
            E2[i, pl.ds(8 + odd, ry3, stride=2)] = v[i]
    recv_all(source2_window)
    for j in (0, 1):
        for i in range(G):
            GS[j, i, pl.ds(10, 8)] = GL[i, 0, j, pl.ds(4, 8)]
            GS[j, i, pl.ds(22, 8)] = GL[i, 2, j, pl.ds(0, 8)]
            GS[j, i, pl.ds(14, 12)] = GS[j, i, pl.ds(14, 12)] + GL[i, 1, j, pl.ds(0, 12)]
    k = lane_of((24, LANES)) & 3
    s2 = []
    for i in range(G):
        left = GS[1, i - 1, pl.ds(8, 24)] if i > 0 else 0.0
        right = GS[1, i + 1, pl.ds(8, 24)] if i + 1 < G else 0.0
        s2.append(GS[0, i, pl.ds(8, 24)] + jnp.where(k < 2, left, right))
    v = [C2[7, i] * s2[i] for i in range(G)]
    v = sweep_whole(v, s2, C2, 2)
    v = [v[i] + E2[i, pl.ds(pl.multiple_of(b * 8, 8), 24)] for i in range(G)]
    for _ in range(SWEEPS):
        v = sweep_whole(v, s2, C2, 2)
    for i in range(G):
        V2[i + 1] = v[i]

    for x2 in range(-2, 6):
        k = x2 % 4
        window = V2[g + 1 + x2 // 4]
        one = jnp.where((lane_of(window.shape) & 3) == k, window, 0.0)
        one = one + roll(one, 1 if k in (0, 2) else -1, 1)
        one = one + roll(one, 2 if k in (0, 1) else -2, 1)
        T[x2 + 2, pl.ds(0, 24)] = one
    for x2 in range(-2, 6):
        add = T[x2 + 2, pl.ds(6, 12)]
        for odd in (0, 1):
            T[x2 + 14, pl.ds(odd, 12, stride=2)] = add
    for x2 in range(-2, 6):
        for i in (2 * x2 + 5, 2 * x2 + 6):
            if 2 <= i < 16:
                U1[i, pl.ds(row1, rows1)] = U1[i, pl.ds(row1, rows1)] + T[x2 + 14, pl.ds(0, rows1)]
    sweep(1, U1, V1, S1, Q1, coeffs1, 3, 15, row1, rows1)
    sweep(1, V1, U1, S1, Q1, coeffs1, 4, 14, row1, rows1)

    for p in range(1, 11):
        add = U1[p + 3, pl.ds(6, 20)]
        for odd in (0, 1):
            T[p, pl.ds(odd, 20, stride=2)] = add
    for p in range(1, 11):
        for i in (2 * p, 2 * p + 1):
            U0[i, pl.ds(row0, rows0)] = U0[i, pl.ds(row0, rows0)] + T[p, pl.ds(0, rows0)]
    sweep(0, U0, V0, S0, Q0, coeffs0, 3, 21, row0, rows0)
    sweep(0, V0, out_ref, S0, Q0, coeffs0, 4, 20, HY, Y0, H0, HY)

    sent_all(source1_halo)
    sent_all(source2_window)
    gather_sent()


def in_one_kernel(G, B, right_side, beta):
    level0 = pltpu.VMEM((X0 + 2 * H0, Y0 + 2 * HY, LANES), F32)
    level1 = pltpu.VMEM((X0 // 2 + 2 * H1, Y0 // 2 + 2 * HY, LANES), F32)
    return pl.pallas_call(
        functools.partial(kernel, G, B),
        out_shape=jax.ShapeDtypeStruct(right_side.shape, F32),
        in_specs=[pl.BlockSpec(memory_space=pltpu.HBM)] * 2,
        out_specs=pl.BlockSpec(memory_space=pltpu.VMEM),
        scratch_shapes=[level0] * 9
        + [level1] * 9
        + [
            pltpu.VMEM((36, Y0 + 8, LANES), F32),
            level0,
            level1,
            pltpu.VMEM((8, LANES), F32),
            pltpu.VMEM((2, 16, LANES), F32),
            pltpu.VMEM((8, LANES), F32),
            pltpu.VMEM((8, LANES), F32),
            pltpu.VMEM((G, 24, LANES), F32),
            pltpu.VMEM((2, G, 40, LANES), F32),
            pltpu.VMEM((G, 3, 2, 16, LANES), F32),
            pltpu.VMEM((2, G, 4 * B + 16, LANES), F32),
            pltpu.VMEM((G + 2, 24, LANES), F32),
            pltpu.VMEM((G + 2, 24, LANES), F32),
            pltpu.VMEM((8, G, 24, LANES), F32),
            pltpu.VMEM((8, G, 4 * B, LANES), F32),
            pltpu.VMEM((8, G, 2 * B, LANES), F32),
            pltpu.VMEM((G, 8 * B, LANES), F32),
            pltpu.VMEM((G, 8 * B + 16, LANES), F32),
            pltpu.VMEM((G + 2, 8, LANES), F32),
            pltpu.VMEM((2, G, 4 * B, LANES), F32),
            pltpu.VMEM((2, 2, Y0, LANES), F32),
            pltpu.VMEM((2, X0, 8, LANES), F32),
            pltpu.VMEM((2, 2, Y0 // 2, LANES), F32),
            pltpu.VMEM((2, X0 // 2, 8, LANES), F32),
            pltpu.SemaphoreType.DMA((4, 8)),
            pltpu.SemaphoreType.DMA((4, 8)),
            pltpu.SemaphoreType.DMA((2, 4)),
            pltpu.SemaphoreType.DMA((2, 4)),
            pltpu.SemaphoreType.DMA((2, 3 * G)),
            pltpu.SemaphoreType.DMA((2, 3 * G)),
            pltpu.SemaphoreType.DMA((1,)),
            pltpu.SemaphoreType.DMA((1,)),
            pltpu.SemaphoreType.REGULAR((2,)),
            pltpu.SemaphoreType.DMA((3,)),
        ],
        compiler_params=pltpu.CompilerParams(
            collective_id=0, has_side_effects=True, vmem_limit_bytes=40 * 1024 * 1024
        ),
    )(*(pltpu.with_memory_space_constraint(a, pltpu.HBM) for a in (right_side, beta)))


relax_weight = 2.0 / 3.0


def with_halo(shard, sides, width):
    for axis, dim in sides:
        size, length = (lax.axis_size(axis), shard.shape[dim])
        up = [(i, (i + 1) % size) for i in range(size - 1)]
        down = [(j, i) for i, j in up]
        last = lax.slice_in_dim(shard, length - width, length, axis=dim)
        leading = lax.slice_in_dim(shard, 0, width, axis=dim)
        before = lax.ppermute(last, axis, up)
        after = lax.ppermute(leading, axis, down)
        shard = jnp.concatenate([before, shard, after], axis=dim)
    return shard


def from_partner(block, axis, apart):
    count = lax.axis_size(axis)
    route = []
    for low in range(count):
        high = low | 1 << apart
        if high != low and high < count:
            route += [(low, high), (high, low)]
    return lax.ppermute(block, axis, route)


def pad_zeros(field):
    return jnp.pad(field, 1)


def pad_local(field):
    extended = with_halo(field, (("grp", 0), ("box", 1)), 1)
    return jnp.pad(extended, ((0, 0), (0, 0), (1, 1)))


def face_coeffs(padded_beta):
    face_x = 0.5 * (padded_beta[1:, 1:-1, 1:-1] + padded_beta[:-1, 1:-1, 1:-1])
    face_y = 0.5 * (padded_beta[1:-1, 1:, 1:-1] + padded_beta[1:-1, :-1, 1:-1])
    face_z = 0.5 * (padded_beta[1:-1, 1:-1, 1:] + padded_beta[1:-1, 1:-1, :-1])
    return (face_x, face_y, face_z)


def inverse_diagonal(coeffs, scale):
    face_x, face_y, face_z = coeffs
    total = (
        face_x[:-1]
        + face_x[1:]
        + face_y[:, :-1]
        + face_y[:, 1:]
        + face_z[:, :, :-1]
        + face_z[:, :, 1:]
    )
    return 1.0 / (scale * total)


def apply_operator(padded, coeffs, scale):
    face_x, face_y, face_z = coeffs
    centre = padded[1:-1, 1:-1, 1:-1]
    total = face_x[:-1] * (centre - padded[:-2, 1:-1, 1:-1]) + face_x[1:] * (
        centre - padded[2:, 1:-1, 1:-1]
    )
    total = (
        total
        + face_y[:, :-1] * (centre - padded[1:-1, :-2, 1:-1])
        + face_y[:, 1:] * (centre - padded[1:-1, 2:, 1:-1])
    )
    total = (
        total
        + face_z[:, :, :-1] * (centre - padded[1:-1, 1:-1, :-2])
        + face_z[:, :, 1:] * (centre - padded[1:-1, 1:-1, 2:])
    )
    return scale * total


def jacobi_sweeps(field, source, coeffs, inverse, scale, count, padder):
    for sweep_index in range(count):
        field = (
            field + relax_weight * (source - apply_operator(padder(field), coeffs, scale)) * inverse
        )
    return field


def conjugate_solve(source, coeffs, scale, count):
    field = jnp.zeros_like(source)
    remain = source
    direction = source
    norm_now = jnp.sum(remain * remain)
    for step_index in range(count):
        image = apply_operator(pad_zeros(direction), coeffs, scale)
        alpha = norm_now / jnp.sum(direction * image)
        field = field + alpha * direction
        remain = remain - alpha * image
        norm_next = jnp.sum(remain * remain)
        direction = remain + norm_next / norm_now * direction
        norm_now = norm_next
    return field


def restrict_mean(field):
    size_a, size_b, size_c = field.shape
    blocks = field.reshape(size_a // 2, 2, size_b // 2, 2, size_c // 2, 2)
    return jnp.mean(blocks, axis=(1, 3, 5))


def prolong_copy(field):
    return jnp.repeat(jnp.repeat(jnp.repeat(field, 2, axis=0), 2, axis=1), 2, axis=2)


def merge_groups(pieces):
    group_index = lax.axis_index("grp")
    for bit_index in range(lax.axis_size("grp").bit_length() - 1):
        partner = from_partner(pieces, "grp", bit_index)
        upper = group_index >> bit_index & 1 == 1
        pieces = tuple(
            (
                jnp.where(
                    upper,
                    jnp.concatenate([theirs, own_piece], 0),
                    jnp.concatenate([own_piece, theirs], 0),
                )
                for own_piece, theirs in zip(pieces, partner)
            )
        )
    return pieces


def merge_boxes(pieces):
    return lax.all_gather(pieces, "box", axis=1, tiled=True)


def shards(right_side, beta):
    source = right_side
    level_beta = beta
    saved = []
    for level in range(LEVELS):
        scale = 0.25**level
        coeffs = face_coeffs(pad_local(level_beta))
        inverse = inverse_diagonal(coeffs, scale)
        field = relax_weight * source * inverse
        field = jacobi_sweeps(field, source, coeffs, inverse, scale, SWEEPS - 1, pad_local)
        residual = source - apply_operator(pad_local(field), coeffs, scale)
        saved.append((field, source, coeffs, inverse, scale))
        source = restrict_mean(residual)
        level_beta = restrict_mean(level_beta)
    low_scale = 0.25**LEVELS
    whole_source, whole_beta = merge_boxes(merge_groups((source, level_beta)))
    low_coeffs = face_coeffs(pad_zeros(whole_beta))
    whole_field = conjugate_solve(whole_source, low_coeffs, low_scale, COARSE)
    block_a, block_b, block_c = source.shape
    field = lax.dynamic_slice(
        whole_field,
        (lax.axis_index("grp") * block_a, lax.axis_index("box") * block_b, 0),
        (block_a, block_b, block_c),
    )
    for level in range(LEVELS - 1, -1, -1):
        kept, level_source, coeffs, inverse, scale = saved[level]
        field = kept + prolong_copy(field)
        field = jacobi_sweeps(field, level_source, coeffs, inverse, scale, SWEEPS, pad_local)
    return field


def solution(mesh):
    placed = P("grp", "box", None)
    G, B = mesh.shape["grp"], mesh.shape["box"]
    small = (G, B) in ((4, 8), (8, 8), (4, 16), (8, 4), (2, 16))

    def local(right_side, beta):
        if small and right_side.shape == (X0, Y0, LANES):
            return in_one_kernel(G, B, right_side, beta)
        return shards(right_side, beta)

    return jax.shard_map(local, mesh=mesh, in_specs=(placed, placed), out_specs=placed, check_vma=False)
```
